256 devices in a mesh: seq: 32 (over z, x), tp: 8 (over y, core).
Axes of the slice: x: 4, y: 4, z: 8, core: 2. Of those that a mesh axis runs over, the one named last changes fastest.
Arguments:
- resp_rows: bfloat16 [512, 16, 5120], P('seq', None, 'tp'), may hold values from -6 to 6
- resp_len: int32 [512], replicated, may hold values from 1 to 16, as said below
- resp_shard: int32 [512, 1], replicated, may hold values from 0 to 31; in each aligned block of 16 rows (0 to 15, 16 to 31, ...) no two rows name the same one
- group_prompt: int32 [32], replicated, may hold values from 0 to 31, each once
- prompt_kv: bfloat16 [2, 32, 256, 1024], P(None, 'seq', None, 'tp'), may hold values from -72 to 72
- w_query: bfloat16 [5120, 3072], P(None, 'tp'), may hold values from -0.078125 to 0.078125
- w_keyval: bfloat16 [2, 5120, 1024], P(None, None, 'tp'), may hold values from -0.078125 to 0.078125
- w_out: bfloat16 [3072, 5120], P('tp'), may hold values from -0.109375 to 0.109375
Outputs:
- attended: bfloat16 [1024, 16, 5120], P('seq', None, 'tp')
The draws below stay inside these ranges and needn't reach their ends.
Inputs may be any that keep to these rules, and one draw needn't show every extreme that they name: `resp_shard`: in the rows of one device (one group) no learner appears more than 1 times, a bound that some block reaches. `group_prompt`: each prompt is answered by exactly one group. `resp_len`: some response has the full 16 tokens.
All inputs are finite; a program needn't handle non-finite values.
Results may differ from the reference program's by a relative error of at most 0.018.
Values may be sent and summed in bfloat16 or wider, within the bound.
No kernel may reach another device: no remote copies, remote signals or barrier semaphores. Data moves between devices by JAX's collectives and lax.ppermute only.
A program may use at most 128 MiB of HBM per device.

```python
import math
import jax
import jax.numpy as jnp
import numpy as np
from jax import lax

D = 5120
HEADS = 24
KVH = 8
HD = 128
PL = 256
RMAX = 16
RESP_DEV = 16
CAP = 1
SLOTS = 32
PROMPTS = 32
RESPONSES = 512
N_SEQ = 32
N_TP = 8


def draw_resp_len(key, part):
    key = jax.random.fold_in(key, 7)
    first_key, second_key, third_key = jax.random.split(key, 3)
    first = jax.random.randint(first_key, (RESPONSES,), 1, RMAX + 1)
    second = jax.random.randint(second_key, (RESPONSES,), 1, RMAX + 1)
    lengths = (first * second + RMAX - 1) // RMAX
    spot = jax.random.randint(third_key, (), 0, RESPONSES)
    return jnp.where(jnp.arange(RESPONSES) == spot, RMAX, lengths).astype(jnp.int32)


def draw_prompt_kv(key, part):
    key = jax.random.fold_in(key, 11)
    base_key = jax.random.fold_in(key, 0)
    cache = jax.random.truncated_normal(base_key, -6.0, 6.0, (2, PROMPTS, PL, KVH * HD), jnp.float32)
    return cache.astype(jnp.bfloat16)


def block_scale(rng, dims, pieces, least, largest):
    def one(dim, shards_of):
        steps = jax.random.uniform(jax.random.fold_in(jax.random.fold_in(rng, 6), dim), (shards_of,), jnp.float32, least / len(pieces), largest / len(pieces))
        return jnp.repeat(jnp.exp(steps), dims[dim] // shards_of).reshape((-1,) + (1,) * (len(dims) - dim - 1))

    loudness = one(*pieces[0])
    for cut in pieces[1:]:
        loudness = loudness * one(*cut)
    return loudness


def deal_out(rng, own, number, rows, number_of, top, reach, slope):
    ranking = jax.random.permutation(rng, number_of)
    packed, usual = portions_of(number_of, rows * top, reach, slope, True), portions_of(number_of, rows * top, reach, slope, False)
    places = jnp.arange(number_of)

    def named(tallies, rotation):
        used = int((tallies > 0).sum())
        fixed = max(1, used // 4)
        shifted = fixed + (places - fixed + rotation * (used - fixed)) % max(1, number_of - fixed)
        return jnp.zeros((number_of,), jnp.int32).at[ranking[jnp.where(places < fixed, places, shifted)]].set(jnp.asarray(tallies, jnp.int32))

    tallies = jnp.where(number % 4 == 0, named(packed, number // 4), named(usual, number - number // 4 - 1))
    mixed = jax.random.permutation(jax.random.fold_in(own, 3), number_of)
    source_of, taker = mixed[0:number_of // 2 * 2:2], mixed[1:number_of // 2 * 2:2]
    room = jnp.minimum(tallies[source_of] - 1, reach - tallies[taker]) // 2
    room = jnp.where((source_of == ranking[0]) | (taker == ranking[0]) | (tallies[taker] == 0), 0, jnp.maximum(room, 0))
    shifted = jax.random.randint(jax.random.fold_in(own, 4), (number_of // 2,), 0, 1 << 20) % (room + 1)
    tallies = tallies.at[source_of].add(-shifted).at[taker].add(shifted)
    members = jnp.searchsorted(jnp.cumsum(tallies), jnp.arange(rows * top), side="right").astype(jnp.int32)
    listing = members.reshape(top, rows).T
    listing = listing[jax.random.permutation(jax.random.fold_in(own, 1), rows)]
    rotation = jax.random.randint(jax.random.fold_in(own, 2), (rows, 1), 0, top)
    return jnp.take_along_axis(listing, (jnp.arange(top)[None, :] + rotation) % top, axis=1)


def portions_of(count, total, most, lean, full):
    loads = [(1 << 20) // math.isqrt(standing ** lean) + 1 for standing in range(1, count + 1)]
    largest = most if full else min(most, max(-(-total // count), total * loads[0] // sum(loads)))
    least = 1 if total - largest >= count - 1 else 0
    holding, surplus = [largest] + [least] * (count - 1), total - largest - least * (count - 1)
    while surplus > 0:
        free = [i for i in range(1, count) if holding[i] < largest] or [i for i in range(1, count) if holding[i] < most]
        mass, remaining = sum([loads[i] for i in free]), surplus
        for i in free:
            more = min(most - holding[i], max(1, remaining * loads[i] // mass), surplus)
            holding[i] = holding[i] + more
            surplus = surplus - more
    return np.array(holding)


def gaussian(stream_key, shape, deviation, reach, shards=(), kind=jnp.bfloat16):
    level = block_scale(stream_key, shape, shards, -0.22, 0.18) if shards else 1.0
    result = jax.random.normal(stream_key, shape, jnp.float32) * deviation * level
    return jnp.minimum(jnp.maximum(result, -reach), reach).astype(kind)


def setup_inputs(seed: int = 0) -> dict:
    key_of = jax.random.split(jax.random.key(seed), 9)
    resp_rows = gaussian(key_of[0], (RESPONSES, RMAX, D), 1.0, 6.0, ((0, 32), (2, 8)))
    resp_len = draw_resp_len(jax.random.fold_in(key_of[8], 71), 0)
    resp_shard_keys = jax.random.split(jax.random.fold_in(key_of[2], 1), RESPONSES // RESP_DEV)
    resp_shard_turns = jax.random.permutation(jax.random.fold_in(key_of[2], 3), RESPONSES // RESP_DEV)
    resp_shard = jax.vmap(lambda own, number: deal_out(jax.random.fold_in(key_of[2], 2), own, number, RESP_DEV, N_SEQ, 1, CAP, 2))(resp_shard_keys, resp_shard_turns).reshape((RESPONSES, 1))
    group_prompt = jax.random.permutation(key_of[3], PROMPTS).astype(jnp.int32)
    prompt_kv = draw_prompt_kv(jax.random.fold_in(key_of[8], 71), 0)
    w_query = gaussian(key_of[5], (D, HEADS * HD), D ** -0.5, 0.078125, ((1, 8),))
    w_keyval = gaussian(key_of[6], (2, D, KVH * HD), D ** -0.5, 0.078125, ((2, 8),))
    w_out = gaussian(key_of[7], (HEADS * HD, D), (HEADS * HD) ** -0.5, 0.109375, ((0, 8),))
    return dict(resp_rows=resp_rows, resp_len=resp_len, resp_shard=resp_shard, group_prompt=group_prompt, prompt_kv=prompt_kv, w_query=w_query, w_keyval=w_keyval, w_out=w_out)


ROPE_BASE = 1000000.0

def rope_tables(count, width, offset):
    places = (offset + jnp.arange(count)).astype(jnp.float32)
    freqs = ROPE_BASE ** (-(jnp.arange(width // 2).astype(jnp.float32) * 2.0 / width))
    angles = places[:, None] * freqs[None, :]
    return (jnp.cos(angles), jnp.sin(angles))

def rotate(values, cosine, sine):
    half = values.shape[-1] // 2
    first = values[..., :half]
    second = values[..., half:]
    cosine = cosine[:, None, :]
    sine = sine[:, None, :]
    return jnp.concatenate([first * cosine - second * sine, second * cosine + first * sine], -1)

def attend(queries, own_keys, own_values, cached_keys, cached_values, lengths):
    scale = 1.0 / math.sqrt(queries.shape[-1])
    prior = jnp.einsum('stkrh,spkh->skrtp', queries.astype(jnp.float32), cached_keys.astype(jnp.float32)) * scale
    recent = jnp.einsum('stkrh,sukh->skrtu', queries.astype(jnp.float32), own_keys.astype(jnp.float32)) * scale
    places = jnp.arange(queries.shape[1])
    causal = places[:, None] >= places[None, :]
    recent = jnp.where(causal, recent, -1e+30)
    top = jnp.maximum(lax.optimization_barrier(jnp.max(prior, -1)), lax.optimization_barrier(jnp.max(recent, -1)))
    prior_exp = jnp.exp(prior - top[..., None])
    recent_exp = jnp.exp(recent - top[..., None])
    total = lax.optimization_barrier(jnp.sum(prior_exp, -1)) + lax.optimization_barrier(jnp.sum(recent_exp, -1))
    prior_w = (prior_exp / total[..., None]).astype(jnp.bfloat16)
    recent_w = (recent_exp / total[..., None]).astype(jnp.bfloat16)
    mixed = jnp.einsum('skrtp,spkh->stkrh', prior_w.astype(jnp.float32), cached_values.astype(jnp.float32))
    mixed = mixed + jnp.einsum('skrtu,sukh->stkrh', recent_w.astype(jnp.float32), own_values.astype(jnp.float32))
    valid = places[None, :] < lengths[:, None]
    mixed = jnp.where(valid[:, :, None, None, None], mixed, 0.0)
    return mixed.astype(jnp.bfloat16).reshape(queries.shape[0], queries.shape[1], -1)

def group_output(rows, cache, lengths, w_query, w_keyval, w_out):
    ratio = HEADS // KVH
    flat = rows.reshape(-1, D)
    cosine, sine = rope_tables(RMAX, HD, PL)
    queries = jnp.dot(flat, w_query, preferred_element_type=jnp.float32).reshape(RESP_DEV, RMAX, HEADS, HD)
    queries = rotate(queries, cosine, sine).astype(jnp.bfloat16).reshape(RESP_DEV, RMAX, KVH, ratio, HD)
    keys = jnp.dot(flat, w_keyval[0], preferred_element_type=jnp.float32).reshape(RESP_DEV, RMAX, KVH, HD)
    keys = rotate(keys, cosine, sine).astype(jnp.bfloat16)
    values = jnp.dot(flat, w_keyval[1], preferred_element_type=jnp.float32).astype(jnp.bfloat16).reshape(RESP_DEV, RMAX, KVH, HD)
    cached_keys = jnp.broadcast_to(cache[0].reshape(1, PL, KVH, HD), (RESP_DEV, PL, KVH, HD))
    cached_values = jnp.broadcast_to(cache[1].reshape(1, PL, KVH, HD), (RESP_DEV, PL, KVH, HD))
    attn = attend(queries, keys, values, cached_keys, cached_values, lengths).reshape(-1, HEADS * HD)
    width = HEADS * HD // N_TP
    total = jnp.zeros((RESP_DEV * RMAX, D), jnp.float32)
    for group in range(N_TP):
        partial_value = jnp.dot(attn[:, group * width:(group + 1) * width], w_out[group * width:(group + 1) * width], preferred_element_type=jnp.float32).astype(jnp.bfloat16)
        total = total + lax.optimization_barrier(partial_value).astype(jnp.float32)
    return total.astype(jnp.bfloat16).reshape(RESP_DEV, RMAX, D)

def reference(resp_rows, resp_len, resp_shard, group_prompt, prompt_kv, w_query, w_keyval, w_out):

    def one_group(items):
        rows, lengths, prompt = items
        cache = jnp.take(prompt_kv, prompt, axis=1)
        return group_output(rows, cache, lengths, w_query, w_keyval, w_out)
    outputs = lax.map(one_group, (resp_rows.reshape(N_SEQ, RESP_DEV, RMAX, D), resp_len.reshape(N_SEQ, RESP_DEV), group_prompt))
    table = resp_shard[:, 0].reshape(N_SEQ, RESP_DEV)
    same = table[:, :, None] == table[:, None, :]
    before = jnp.arange(RESP_DEV)[None, :] < jnp.arange(RESP_DEV)[:, None]
    rank = lax.optimization_barrier(jnp.sum((same & before[None, :, :]).astype(jnp.int32), -1))
    slot = table * SLOTS + jnp.arange(N_SEQ).astype(jnp.int32)[:, None] * CAP + rank
    attended = jnp.zeros((N_SEQ * SLOTS, RMAX, D), jnp.bfloat16)
    return attended.at[slot.reshape(-1).astype(jnp.int32)].set(outputs.reshape(RESPONSES, RMAX, D))
```

```python
import functools
import math

import jax
import jax.numpy as jnp
from jax import lax
from jax.experimental import pallas as pl
from jax.experimental.pallas import tpu as pltpu
from jax.sharding import PartitionSpec as P

HD = 128
PL = 256
ROPE_BASE = 1000000.0
CHIPS = 4
CORES = 2


def chip_shift(step):
    return [
        (y * CORES + c, ((y + step) % CHIPS) * CORES + c) for y in range(CHIPS) for c in range(CORES)
    ]


CORE_SWAP = [(i, i ^ 1) for i in range(CHIPS * CORES)]


def rope_tables(count, rows):
    places = (PL + jnp.arange(count)).astype(jnp.float32)
    freqs = ROPE_BASE ** (-(jnp.arange(HD // 2).astype(jnp.float32) * 2.0 / HD))
    angles = places[:, None] * freqs[None, :]
    cosine, sine = jnp.cos(angles), jnp.sin(angles)
    cosine = jnp.concatenate([cosine, cosine], -1)
    sine = jnp.concatenate([-sine, sine], -1)
    return jnp.tile(cosine, (rows // count, 1)), jnp.tile(sine, (rows // count, 1))


def group_kernel(
    heads,
    tokens,
    from_ref,
    to_ref,
    *refs,
):
    xs = refs[:8]
    wq_ref, wkv_ref, cache_ref, cos_ref, sin_ref, valid_ref, wo_ref = refs[8:15]
    other_ref, mine_ref = refs[15:17]
    acc_q, acc_kv, attn = refs[17:]
    step = pl.program_id(0)
    rows = attn.shape[0]

    for k in range(8):

        @pl.when(step == k)
        def _():
            x = xs[k][...]
            q = jnp.dot(x, wq_ref[...], preferred_element_type=jnp.float32)
            keys = jnp.dot(x, wkv_ref[0], preferred_element_type=jnp.float32)
            values = jnp.dot(x, wkv_ref[1], preferred_element_type=jnp.float32)
            if k == 0:
                acc_q[...] = q
                acc_kv[0] = keys
                acc_kv[1] = values
            else:
                acc_q[...] += q
                acc_kv[0] += keys
                acc_kv[1] += values

    @pl.when(step == 7)
    def _():
        cosine, sine = cos_ref[...], sin_ref[...]

        def rotate(v):
            return (v * cosine + pltpu.roll(v, HD // 2, 1) * sine).astype(jnp.bfloat16)

        scale = 1.0 / math.sqrt(HD)
        own_keys = rotate(acc_kv[0])
        own_values = acc_kv[1].astype(jnp.bfloat16)
        half = cache_ref.shape[0] // 2
        cached_keys = cache_ref[:half].reshape(PL, HD)
        cached_values = cache_ref[half:].reshape(PL, HD)
        row = lax.broadcasted_iota(jnp.int32, (rows, rows), 0)
        col = lax.broadcasted_iota(jnp.int32, (rows, rows), 1)
        seen = (row // tokens == col // tokens) & (col <= row)
        nt = (((1,), (1,)), ((), ()))
        for h in range(heads):
            q = rotate(acc_q[:, h * HD : (h + 1) * HD])
            prior = lax.dot_general(q, cached_keys, nt, preferred_element_type=jnp.float32) * scale
            recent = lax.dot_general(q, own_keys, nt, preferred_element_type=jnp.float32) * scale
            recent = jnp.where(seen, recent, -1e30)
            top = jnp.maximum(
                jnp.max(prior, -1, keepdims=True), jnp.max(recent, -1, keepdims=True)
            )
            prior = jnp.exp(prior - top)
            recent = jnp.exp(recent - top)
            total = jnp.sum(prior, -1, keepdims=True) + jnp.sum(recent, -1, keepdims=True)
            inverse = 1.0 / total
            prior = (prior * inverse).astype(jnp.bfloat16)
            recent = (recent * inverse).astype(jnp.bfloat16)
            mixed = jnp.dot(prior, cached_values, preferred_element_type=jnp.float32)
            mixed += jnp.dot(recent, own_values, preferred_element_type=jnp.float32)
            mixed = jnp.where(valid_ref[...] > 0.0, mixed, 0.0)
            attn[:, h * HD : (h + 1) * HD] = mixed.astype(jnp.bfloat16)

    @pl.when((step >= 8) & (step < 12))
    def _():
        other_ref[0] = jnp.dot(
            attn[...], wo_ref[...], preferred_element_type=jnp.float32
        ).astype(jnp.bfloat16)

    @pl.when(step >= 12)
    def _():
        mine_ref[0] = jnp.dot(
            attn[...], wo_ref[...], preferred_element_type=jnp.float32
        ).astype(jnp.bfloat16)


def group_call(order_from, order_to, shards, w_query, w_keyval, cache, cosine, sine, valid, w_out, tokens):
    rows, width = shards[0].shape
    q_width = w_query.shape[1]
    heads = q_width // HD
    whole = lambda a: pl.BlockSpec(a.shape, lambda i, f, t, n=a.ndim: (0,) * n)
    grid_spec = pltpu.PrefetchScalarGridSpec(
        num_scalar_prefetch=2,
        grid=(16,),
        in_specs=[whole(x) for x in shards]
        + [
            pl.BlockSpec((width, q_width), lambda i, f, t: (f[jnp.minimum(i, 7)], 0)),
            pl.BlockSpec((2, width, HD), lambda i, f, t: (0, f[jnp.minimum(i, 7)], 0)),
            whole(cache),
            whole(cosine),
            whole(sine),
            whole(valid),
            pl.BlockSpec((q_width, width), lambda i, f, t: (0, t[jnp.maximum(i - 8, 0)])),
        ],
        out_specs=[
            pl.BlockSpec((1, rows, width), lambda i, f, t: (jnp.clip(i - 8, 0, 3), 0, 0)),
            pl.BlockSpec((1, rows, width), lambda i, f, t: (jnp.clip(i - 12, 0, 3), 0, 0)),
        ],
        scratch_shapes=[
            pltpu.VMEM((rows, q_width), jnp.float32),
            pltpu.VMEM((2, rows, HD), jnp.float32),
            pltpu.VMEM((rows, q_width), jnp.bfloat16),
        ],
    )
    block = jax.ShapeDtypeStruct((4, rows, width), jnp.bfloat16)
    return pl.pallas_call(
        functools.partial(group_kernel, heads, tokens),
        grid_spec=grid_spec,
        out_shape=[block, block],
        compiler_params=pltpu.CompilerParams(
            dimension_semantics=("arbitrary",), vmem_limit_bytes=32 * 1024 * 1024
        ),
        cost_estimate=pl.CostEstimate(
            flops=3_000_000_000, bytes_accessed=16_000_000, transcendentals=400_000
        ),
    )(order_from, order_to, *shards, w_query, w_keyval, cache, cosine, sine, valid, w_out)


def per_device(resp_rows, resp_len, resp_shard, group_prompt, prompt_kv, w_query, w_keyval, w_out):
    learners = lax.axis_size("seq")
    group = lax.axis_index("seq")
    me = lax.axis_index("tp")
    y, c = me // CORES, me % CORES
    group_size, tokens, width = resp_rows.shape
    rows = group_size * tokens

    pieces = prompt_kv.reshape(learners, -1, HD)
    pieces = lax.all_to_all(pieces, "seq", 0, 0, tiled=True)
    pieces = jnp.take(pieces, group_prompt, axis=0)
    cache = lax.all_to_all(pieces, "seq", 0, 0, tiled=True)

    x = resp_rows.reshape(rows, width)
    below = lax.ppermute(x, "tp", chip_shift(1))
    above = lax.ppermute(x, "tp", chip_shift(-1))
    across = lax.ppermute(x, "tp", chip_shift(2))
    near = [x, below, above, across]
    far = [lax.ppermute(v, "tp", CORE_SWAP) for v in near]

    def places(shifts):
        at = jnp.stack([(y + s) % CHIPS for s in shifts])
        return jnp.concatenate([at * CORES + c, at * CORES + 1 - c]).astype(jnp.int32)

    order_from = places((0, -1, 1, 2))
    order_to = places((0, 1, -1, 2))
    order_to = jnp.concatenate([order_to[4:], order_to[:4]])

    own_len = lax.dynamic_slice_in_dim(resp_len, group * group_size, group_size, 0)
    valid = (jnp.arange(tokens)[None, :] < own_len[:, None]).astype(jnp.float32)
    valid = jnp.broadcast_to(valid.reshape(rows, 1), (rows, HD))
    cosine, sine = rope_tables(tokens, rows)

    other, mine = group_call(
        order_from, order_to, near + far, w_query, w_keyval, cache, cosine, sine, valid, w_out, tokens
    )
    other = lax.ppermute(other, "tp", CORE_SWAP)
    both = mine.astype(jnp.float32) + other.astype(jnp.float32)
    sent = both[1:].astype(jnp.bfloat16)
    parts = [
        lax.ppermute(sent[0], "tp", chip_shift(1)),
        lax.ppermute(sent[1], "tp", chip_shift(-1)),
        lax.ppermute(sent[2], "tp", chip_shift(2)),
    ]
    total = both[0]
    for part in parts:
        total = total + part.astype(jnp.float32)
    total = total.astype(jnp.bfloat16).reshape(group_size, tokens, width)

    own_shard = lax.dynamic_slice_in_dim(resp_shard[:, 0], group * group_size, group_size, 0)
    match = own_shard[None, :] == jnp.arange(learners)[:, None]
    pick = jnp.sum(jnp.where(match, jnp.arange(group_size)[None, :], 0), -1)
    filled = jnp.any(match, -1)
    slots = jnp.where(filled[:, None, None], jnp.take(total, pick, axis=0), 0)
    return lax.all_to_all(slots.astype(jnp.bfloat16), "seq", 0, 0, tiled=True)


def solution(mesh):
    return jax.shard_map(
        per_device,
        mesh=mesh,
        in_specs=(
            P("seq", None, "tp"),
            P(),
            P(),
            P(),
            P(None, "seq", None, "tp"),
            P(None, "tp"),
            P(None, None, "tp"),
            P("tp", None),
        ),
        out_specs=P("seq", None, "tp"),
        check_vma=False,
    )
```

```python
import functools
import math

import jax
import jax.numpy as jnp
from jax import lax
from jax.experimental import pallas as pl
from jax.experimental.pallas import tpu as pltpu
from jax.sharding import PartitionSpec as P

HD = 128
PL = 256
ROPE_BASE = 1000000.0
CHIPS = 4
CORES = 2


def chip_shift(step):
    return [
        (y * CORES + c, ((y + step) % CHIPS) * CORES + c) for y in range(CHIPS) for c in range(CORES)
    ]


CORE_SWAP = [(i, i ^ 1) for i in range(CHIPS * CORES)]


def rope_tables(count, rows):
    places = (PL + jnp.arange(count)).astype(jnp.float32)
    freqs = ROPE_BASE ** (-(jnp.arange(HD // 2).astype(jnp.float32) * 2.0 / HD))
    angles = places[:, None] * freqs[None, :]
    cosine, sine = jnp.cos(angles), jnp.sin(angles)
    cosine = jnp.concatenate([cosine, cosine], -1)
    sine = jnp.concatenate([-sine, sine], -1)
    return jnp.tile(cosine, (rows // count, 1)), jnp.tile(sine, (rows // count, 1))


VMEM = pl.BlockSpec(memory_space=pltpu.VMEM)
SMEM = pl.BlockSpec(memory_space=pltpu.SMEM)
ANY = pl.BlockSpec(memory_space=pl.ANY)


def in_hbm(x):
    return pltpu.with_memory_space_constraint(x, pltpu.HBM)


def params(mib):
    return pltpu.CompilerParams(vmem_limit_bytes=mib * 1024 * 1024)


def place_in_column(shifts, far):
    me = lax.axis_index("tp")
    y, c = me // CORES, me % CORES
    core = 1 - c if far else c
    return [((y + shift + CHIPS) % CHIPS) * CORES + core for shift in shifts]


def columns_at(index, width):
    return pl.ds(pl.multiple_of(index * width, width), width)


def route_kernel(pick_ref, piece_ref, out_ref):
    count, size, width = piece_ref.shape
    pieces = piece_ref[...].reshape(count * size, width)
    picked = jnp.dot(pick_ref[...], pieces, preferred_element_type=jnp.float32)
    out_ref[...] = picked.astype(jnp.bfloat16).reshape(count, size, width)


def route(pick, pieces):
    return pl.pallas_call(
        route_kernel,
        in_specs=[VMEM, VMEM],
        out_specs=VMEM,
        out_shape=jax.ShapeDtypeStruct(pieces.shape, pieces.dtype),
        compiler_params=params(8),
    )(pick, pieces)


def weight_row_copies(i, index, wq_hbm, wkv_hbm, weights, sems):
    width = weights.shape[1]
    first = wq_hbm.shape[1]
    at = columns_at(index, width)
    return (
        pltpu.make_async_copy(wq_hbm.at[at, :], weights.at[i, :, 0:first], sems.at[0, i]),
        pltpu.make_async_copy(
            wkv_hbm.at[0, at, :], weights.at[i, :, first : first + HD], sems.at[1, i]
        ),
        pltpu.make_async_copy(
            wkv_hbm.at[1, at, :], weights.at[i, :, first + HD : first + 2 * HD], sems.at[2, i]
        ),
    )


def project_pairs(rows_ref, weights, copies):
    _, width, columns = weights.shape
    total = None
    for pair in range(len(copies) // 2):
        for copy in copies[2 * pair] + copies[2 * pair + 1]:
            copy.wait()
        part = jnp.dot(
            rows_ref[:, 2 * pair * width : 2 * (pair + 1) * width],
            weights[2 * pair : 2 * (pair + 1)].reshape(2 * width, columns),
            preferred_element_type=jnp.float32,
        )
        total = part if total is None else total + part
    return total


def project_kernel(x_hbm, *refs):
    shards = refs[:7]
    wq_hbm, wkv_hbm, cos_ref, sin_ref = refs[7:11]
    q_ref, k_ref, v_ref, rows_ref, weights, sems, x_sem = refs[11:]
    width = weights.shape[1]
    heads = q_ref.shape[0]
    near = place_in_column((0, -1, 1, 2), False)
    far = place_in_column((0, -1, 1, 2), True)
    order = [index for pair in zip(near, far) for index in pair]
    own = pltpu.make_async_copy(x_hbm, rows_ref.at[:, 0:width], x_sem)
    own.start()
    copies = [
        weight_row_copies(i, index, wq_hbm, wkv_hbm, weights, sems) for i, index in enumerate(order)
    ]
    for triple in copies:
        for copy in triple:
            copy.start()
    for i, shard in enumerate(shards):
        rows_ref[:, (i + 1) * width : (i + 2) * width] = shard[...]
    own.wait()
    both = project_pairs(rows_ref, weights, copies)
    cosine, sine = cos_ref[...], sin_ref[...]

    def rotated(h):
        v = both[:, h * HD : (h + 1) * HD]
        return (v * cosine + pltpu.roll(v, HD // 2, 1) * sine).astype(jnp.bfloat16)

    for h in range(heads):
        q_ref[h] = rotated(h)
    k_ref[...] = rotated(heads)
    v_ref[...] = both[:, (heads + 1) * HD :].astype(jnp.bfloat16)


def project(x, shards, w_query, w_keyval, cosine, sine):
    rows, width = x.shape
    heads = w_query.shape[1] // HD
    columns = (heads + 2) * HD
    return pl.pallas_call(
        project_kernel,
        in_specs=[ANY] + [VMEM] * 7 + [ANY] * 2 + [VMEM] * 2,
        out_specs=[VMEM] * 3,
        out_shape=[
            jax.ShapeDtypeStruct((heads, rows, HD), jnp.bfloat16),
            jax.ShapeDtypeStruct((rows, HD), jnp.bfloat16),
            jax.ShapeDtypeStruct((rows, HD), jnp.bfloat16),
        ],
        scratch_shapes=[
            pltpu.VMEM((rows, 8 * width), jnp.bfloat16),
            pltpu.VMEM((8, width, columns), jnp.bfloat16),
            pltpu.SemaphoreType.DMA((3, 8)),
            pltpu.SemaphoreType.DMA,
        ],
        compiler_params=params(16),
        cost_estimate=pl.CostEstimate(
            flops=2 * rows * 8 * width * columns,
            bytes_accessed=16 * width * columns,
            transcendentals=0,
        ),
    )(in_hbm(x), *shards, in_hbm(w_query), in_hbm(w_keyval), cosine, sine)


def out_weight_copies(i, shift, near_hbm, far_hbm, wo_ref, sems):
    depth = near_hbm.shape[0]
    at = columns_at(place_in_column((shift,), False)[0], wo_ref.shape[2])
    return (
        pltpu.make_async_copy(near_hbm.at[:, at], wo_ref.at[i, 0:depth, :], sems.at[0, i]),
        pltpu.make_async_copy(far_hbm.at[:, at], wo_ref.at[i, depth : 2 * depth, :], sems.at[1, i]),
    )


def attend_kernel(
    tokens,
    shift,
    q_ref,
    k_ref,
    v_ref,
    cache_ref,
    valid_ref,
    near_hbm,
    far_hbm,
    attn_ref,
    wo_ref,
    sems,
):
    copies = out_weight_copies(0, shift, near_hbm, far_hbm, wo_ref, sems)
    for copy in copies:
        copy.start()
    heads, rows, _ = q_ref.shape
    scale = 1.0 / math.sqrt(HD)
    half = cache_ref.shape[0] // 2
    keys = jnp.concatenate([cache_ref[:half].reshape(PL, HD), k_ref[...]], 0)
    values = jnp.concatenate([cache_ref[half:].reshape(PL, HD), v_ref[...]], 0)
    row = lax.broadcasted_iota(jnp.int32, (rows, rows), 0)
    col = lax.broadcasted_iota(jnp.int32, (rows, rows), 1)
    seen = (row // tokens == col // tokens) & (col <= row)
    valid = valid_ref[...] > 0.0
    nt = (((1,), (1,)), ((), ()))
    scores = [
        lax.dot_general(q_ref[h], keys, nt, preferred_element_type=jnp.float32) * scale
        for h in range(heads)
    ]
    for h in range(heads):
        prior = scores[h][:, :PL]
        recent = jnp.where(seen, scores[h][:, PL:], -1e30)
        top = jnp.max(jnp.maximum(prior, recent), -1, keepdims=True)
        prior = jnp.exp(prior - top)
        recent = jnp.exp(recent - top)
        inverse = 1.0 / jnp.sum(prior + recent, -1, keepdims=True)
        weights = jnp.concatenate(
            [(prior * inverse).astype(jnp.bfloat16), (recent * inverse).astype(jnp.bfloat16)], -1
        )
        mixed = jnp.dot(weights, values, preferred_element_type=jnp.float32)
        attn_ref[:, h * HD : (h + 1) * HD] = jnp.where(valid, mixed, 0.0).astype(jnp.bfloat16)
    for copy in copies:
        copy.wait()


def attend(shift, queries, keys, values, cache, valid, out_near, out_far, tokens):
    heads, rows, _ = queries.shape
    depth, width = out_near.shape[0], out_near.shape[1] // (CHIPS * CORES)
    return pl.pallas_call(
        functools.partial(attend_kernel, tokens, shift),
        in_specs=[VMEM] * 5 + [ANY] * 2,
        out_specs=[VMEM] * 2,
        out_shape=[
            jax.ShapeDtypeStruct((rows, heads * HD), jnp.bfloat16),
            jax.ShapeDtypeStruct((1, 2 * depth, width), jnp.bfloat16),
        ],
        scratch_shapes=[pltpu.SemaphoreType.DMA((2, 1))],
        compiler_params=params(8),
        cost_estimate=pl.CostEstimate(
            flops=8 * heads * rows * PL * HD,
            bytes_accessed=4 * rows * heads * HD + 4 * depth * width,
            transcendentals=2 * heads * rows * PL,
        ),
    )(queries, keys, values, cache, valid, in_hbm(out_near), in_hbm(out_far))


def fetch_kernel(shift, after_ref, near_hbm, far_hbm, wo_ref, sems):
    del after_ref
    copies = out_weight_copies(0, shift, near_hbm, far_hbm, wo_ref, sems)
    for copy in copies:
        copy.start()
    for copy in copies:
        copy.wait()


def fetch(shift, after, out_near, out_far):
    depth, width = out_near.shape[0], out_near.shape[1] // (CHIPS * CORES)
    return pl.pallas_call(
        functools.partial(fetch_kernel, shift),
        in_specs=[ANY] * 3,
        out_specs=VMEM,
        out_shape=jax.ShapeDtypeStruct((1, 2 * depth, width), jnp.bfloat16),
        scratch_shapes=[pltpu.SemaphoreType.DMA((2, 1))],
        compiler_params=params(8),
        cost_estimate=pl.CostEstimate(
            flops=0, bytes_accessed=8 * depth * width, transcendentals=0
        ),
    )(after, in_hbm(out_near), in_hbm(out_far))


def output_kernel(ready, shifts, near_ref, far_ref, *refs):
    ready_refs = refs[:ready]
    refs = refs[ready:]
    copies = []
    if shifts:
        near_hbm, far_hbm = refs[:2]
        wo_ref, sems = refs[-2:]
        refs = refs[2:-2]
        copies = [
            out_weight_copies(i, shift, near_hbm, far_hbm, wo_ref, sems)
            for i, shift in enumerate(shifts)
        ]
    for pair in copies:
        for copy in pair:
            copy.start()
    both = jnp.concatenate([near_ref[...], far_ref[...]], -1)
    for i, out_ref in enumerate(refs):
        if i < ready:
            weights = ready_refs[i][0]
        else:
            for copy in copies[i - ready]:
                copy.wait()
            weights = wo_ref[i - ready]
        block = jnp.dot(both, weights, preferred_element_type=jnp.float32)
        out_ref[...] = block.astype(out_ref.dtype)


def output(near, far, ready, shifts, out_near, out_far, dtype):
    rows = near.shape[0]
    depth, width = out_near.shape[0], out_near.shape[1] // (CHIPS * CORES)
    count = len(ready) + len(shifts)
    hbm = [in_hbm(out_near), in_hbm(out_far)] if shifts else []
    scratch = [
        pltpu.VMEM((len(shifts), 2 * depth, width), jnp.bfloat16),
        pltpu.SemaphoreType.DMA((2, len(shifts))),
    ]
    return pl.pallas_call(
        functools.partial(output_kernel, len(ready), shifts),
        in_specs=[VMEM] * (2 + len(ready)) + [ANY] * len(hbm),
        out_specs=[VMEM] * count,
        out_shape=[jax.ShapeDtypeStruct((rows, width), dtype)] * count,
        scratch_shapes=scratch if shifts else [],
        compiler_params=params(8),
        cost_estimate=pl.CostEstimate(
            flops=4 * count * rows * depth * width,
            bytes_accessed=4 * count * depth * width,
            transcendentals=0,
        ),
    )(near, far, *ready, *hbm)


def place_kernel(pick_ref, mine_ref, *refs):
    parts, out_ref = refs[:3], refs[3]
    total = mine_ref[...]
    for part in parts:
        total = total + part[...].astype(jnp.float32)
    placed = jnp.dot(
        pick_ref[...], total.astype(jnp.bfloat16), preferred_element_type=jnp.float32
    )
    out_ref[...] = placed.astype(jnp.bfloat16).reshape(out_ref.shape)


def place(pick, mine, parts, slots, tokens):
    _, width = mine.shape
    return pl.pallas_call(
        place_kernel,
        in_specs=[VMEM] * 5,
        out_specs=VMEM,
        out_shape=jax.ShapeDtypeStruct((slots, tokens, width), jnp.bfloat16),
        compiler_params=params(8),
    )(pick, mine, *parts)


def block_picks(source, size, count):
    rows = source[:, None] * size + jnp.arange(size)[None, :]
    rows = jnp.where(source[:, None] >= 0, rows, -1).reshape(-1)
    return (rows[:, None] == jnp.arange(count * size)[None, :]).astype(jnp.bfloat16)


def per_device(resp_rows, resp_len, resp_shard, group_prompt, prompt_kv, w_query, w_keyval, w_out):
    learners = lax.axis_size("seq")
    group = lax.axis_index("seq")
    group_size, tokens, width = resp_rows.shape
    rows = group_size * tokens

    pieces = prompt_kv.reshape(learners, -1, HD)
    prompt_picks = block_picks(group_prompt, pieces.shape[1], learners)
    pieces = lax.all_to_all(pieces, "seq", 0, 0, tiled=True)

    x = resp_rows.reshape(rows, width)
    swap = lambda v: lax.ppermute(v, "tp", CORE_SWAP)
    below = lax.ppermute(x, "tp", chip_shift(1))
    above = lax.ppermute(x, "tp", chip_shift(-1))
    across = lax.ppermute(x, "tp", chip_shift(2))
    cache = lax.all_to_all(route(prompt_picks, pieces), "seq", 0, 0, tiled=True)
    out_far = swap(w_out)
    shards = [swap(x), below, swap(below), above, swap(above), across, swap(across)]

    own_len = lax.dynamic_slice_in_dim(resp_len, group * group_size, group_size, 0)
    valid = (jnp.arange(tokens)[None, :] < own_len[:, None]).astype(jnp.float32)
    valid = jnp.broadcast_to(valid.reshape(rows, 1), (rows, HD))
    cosine, sine = rope_tables(tokens, rows)
    own_shard = lax.dynamic_slice_in_dim(resp_shard[:, 0], group * group_size, group_size, 0)
    match = own_shard[None, :] == jnp.arange(learners)[:, None]
    pick = jnp.max(jnp.where(match, jnp.arange(group_size)[None, :], -1), -1)
    slot_picks = block_picks(pick, tokens, group_size)

    queries, keys, values = project(x, shards, w_query, w_keyval, cosine, sine)
    attn, w_across = attend(2, queries, keys, values, cache, valid, w_out, out_far, tokens)
    attn_far = swap(attn)
    w_above = fetch(1, attn, w_out, out_far)
    (to_across,) = output(attn, attn_far, [w_across], (), w_out, out_far, jnp.bfloat16)
    to_across, attn_far = lax.optimization_barrier((to_across, attn_far))
    to_above, to_below = output(
        attn, attn_far, [w_above], (-1,), w_out, out_far, jnp.bfloat16
    )
    (mine,) = output(attn, attn_far, [], (0,), w_out, out_far, jnp.float32)
    parts = [
        lax.ppermute(to_across, "tp", chip_shift(2)),
        lax.ppermute(to_above, "tp", chip_shift(1)),
        lax.ppermute(to_below, "tp", chip_shift(-1)),
    ]
    slots = place(slot_picks, mine, parts, learners, tokens)
    return lax.all_to_all(slots, "seq", 0, 0, tiled=True)


def solution(mesh):
    return jax.shard_map(
        per_device,
        mesh=mesh,
        in_specs=(
            P("seq", None, "tp"),
            P(),
            P(),
            P(),
            P(None, "seq", None, "tp"),
            P(None, "tp"),
            P(None, None, "tp"),
            P("tp", None),
        ),
        out_specs=P("seq", None, "tp"),
        check_vma=False,
    )
```

```python
import functools
import math

import jax
import jax.numpy as jnp
from jax import lax
from jax.experimental import pallas as pl
from jax.experimental.pallas import tpu as pltpu
from jax.sharding import PartitionSpec as P

HD = 128
PL = 256
ROPE_BASE = 1000000.0
CHIPS = 4
CORES = 2


def chip_shift(step):
    return [
        (y * CORES + c, ((y + step) % CHIPS) * CORES + c) for y in range(CHIPS) for c in range(CORES)
    ]


CORE_SWAP = [(i, i ^ 1) for i in range(CHIPS * CORES)]


def rope_tables(count, rows):
    places = (PL + jnp.arange(count)).astype(jnp.float32)
    freqs = ROPE_BASE ** (-(jnp.arange(HD // 2).astype(jnp.float32) * 2.0 / HD))
    angles = places[:, None] * freqs[None, :]
    cosine, sine = jnp.cos(angles), jnp.sin(angles)
    cosine = jnp.concatenate([cosine, cosine], -1)
    sine = jnp.concatenate([-sine, sine], -1)
    return jnp.tile(cosine, (rows // count, 1)), jnp.tile(sine, (rows // count, 1))


VMEM = pl.BlockSpec(memory_space=pltpu.VMEM)
SMEM = pl.BlockSpec(memory_space=pltpu.SMEM)
ANY = pl.BlockSpec(memory_space=pl.ANY)


def in_hbm(x):
    return pltpu.with_memory_space_constraint(x, pltpu.HBM)


def params(mib):
    return pltpu.CompilerParams(vmem_limit_bytes=mib * 1024 * 1024)


def place_in_column(shifts, far):
    me = lax.axis_index("tp")
    y, c = me // CORES, me % CORES
    core = 1 - c if far else c
    return [((y + shift + CHIPS) % CHIPS) * CORES + core for shift in shifts]


def columns_at(index, width):
    return pl.ds(pl.multiple_of(index * width, width), width)


def route_kernel(pick_ref, piece_ref, out_ref):
    count, size, width = piece_ref.shape
    pieces = piece_ref[...].reshape(count * size, width)
    picked = jnp.dot(pick_ref[...], pieces, preferred_element_type=jnp.float32)
    out_ref[...] = picked.astype(jnp.bfloat16).reshape(count, size, width)


def route(pick, pieces):
    return pl.pallas_call(
        route_kernel,
        in_specs=[VMEM, VMEM],
        out_specs=VMEM,
        out_shape=jax.ShapeDtypeStruct(pieces.shape, pieces.dtype),
        compiler_params=params(8),
    )(pick, pieces)


def weight_row_copies(i, index, wq_hbm, wkv_hbm, weights, sems):
    width = weights.shape[1]
    first = wq_hbm.shape[1]
    at = columns_at(index, width)
    return (
        pltpu.make_async_copy(wq_hbm.at[at, :], weights.at[i, :, 0:first], sems.at[0, i]),
        pltpu.make_async_copy(
            wkv_hbm.at[0, at, :], weights.at[i, :, first : first + HD], sems.at[1, i]
        ),
        pltpu.make_async_copy(
            wkv_hbm.at[1, at, :], weights.at[i, :, first + HD : first + 2 * HD], sems.at[2, i]
        ),
    )


def project_pairs(rows_ref, weights, copies):
    _, width, columns = weights.shape
    total = None
    for pair in range(len(copies) // 2):
        for copy in copies[2 * pair] + copies[2 * pair + 1]:
            copy.wait()
        part = jnp.dot(
            rows_ref[:, 2 * pair * width : 2 * (pair + 1) * width],
            weights[2 * pair : 2 * (pair + 1)].reshape(2 * width, columns),
            preferred_element_type=jnp.float32,
        )
        total = part if total is None else total + part
    return total


def out_weight_copies(i, shift, near_hbm, far_hbm, wo_ref, sems):
    depth = near_hbm.shape[0]
    at = columns_at(place_in_column((shift,), False)[0], wo_ref.shape[2])
    return (
        pltpu.make_async_copy(near_hbm.at[:, at], wo_ref.at[i, 0:depth, :], sems.at[0, i]),
        pltpu.make_async_copy(far_hbm.at[:, at], wo_ref.at[i, depth : 2 * depth, :], sems.at[1, i]),
    )


def project_kernel(x_hbm, *refs):
    shards = refs[:7]
    wq_hbm, wkv_hbm, cos_ref, sin_ref = refs[7:11]
    q_ref, k_ref, v_ref, rows_ref, weights, sems, x_sem = refs[11:]
    width = weights.shape[1]
    heads = q_ref.shape[0]
    near = place_in_column((0, -1, 1, 2), False)
    far = place_in_column((0, -1, 1, 2), True)
    order = [index for pair in zip(near, far) for index in pair]
    own = pltpu.make_async_copy(x_hbm, rows_ref.at[:, 0:width], x_sem)
    own.start()
    copies = [
        weight_row_copies(i, index, wq_hbm, wkv_hbm, weights, sems) for i, index in enumerate(order)
    ]
    for triple in copies:
        for copy in triple:
            copy.start()
    for i, shard in enumerate(shards):
        rows_ref[:, (i + 1) * width : (i + 2) * width] = shard[...]
    own.wait()
    both = project_pairs(rows_ref, weights, copies)
    cosine, sine = cos_ref[...], sin_ref[...]

    def rotated(h):
        v = both[:, h * HD : (h + 1) * HD]
        return (v * cosine + pltpu.roll(v, HD // 2, 1) * sine).astype(jnp.bfloat16)

    for h in range(heads):
        q_ref[h] = rotated(h)
    k_ref[...] = rotated(heads)
    v_ref[...] = both[:, (heads + 1) * HD :].astype(jnp.bfloat16)


def project(x, shards, w_query, w_keyval, cosine, sine):
    rows, width = x.shape
    heads = w_query.shape[1] // HD
    columns = (heads + 2) * HD
    return pl.pallas_call(
        project_kernel,
        in_specs=[ANY] + [VMEM] * 7 + [ANY] * 2 + [VMEM] * 2,
        out_specs=[VMEM] * 3,
        out_shape=[
            jax.ShapeDtypeStruct((heads, rows, HD), jnp.bfloat16),
            jax.ShapeDtypeStruct((rows, HD), jnp.bfloat16),
            jax.ShapeDtypeStruct((rows, HD), jnp.bfloat16),
        ],
        scratch_shapes=[
            pltpu.VMEM((rows, 8 * width), jnp.bfloat16),
            pltpu.VMEM((8, width, columns), jnp.bfloat16),
            pltpu.SemaphoreType.DMA((3, 8)),
            pltpu.SemaphoreType.DMA,
        ],
        compiler_params=params(16),
        cost_estimate=pl.CostEstimate(
            flops=2 * rows * 8 * width * columns,
            bytes_accessed=16 * width * columns,
            transcendentals=0,
        ),
    )(
        in_hbm(x),
        *shards,
        in_hbm(w_query),
        in_hbm(w_keyval),
        cosine,
        sine,
    )


def attend_kernel(tokens, q_ref, k_ref, v_ref, cache_ref, valid_ref, attn_ref):
    heads, rows, _ = q_ref.shape
    scale = 1.0 / math.sqrt(HD)
    half = cache_ref.shape[0] // 2
    keys = jnp.concatenate([cache_ref[:half].reshape(PL, HD), k_ref[...]], 0)
    values = jnp.concatenate([cache_ref[half:].reshape(PL, HD), v_ref[...]], 0)
    row = lax.broadcasted_iota(jnp.int32, (rows, rows), 0)
    col = lax.broadcasted_iota(jnp.int32, (rows, rows), 1)
    seen = (row // tokens == col // tokens) & (col <= row)
    valid = valid_ref[...] > 0.0
    nt = (((1,), (1,)), ((), ()))
    scores = [
        lax.dot_general(q_ref[h], keys, nt, preferred_element_type=jnp.float32) * scale
        for h in range(heads)
    ]
    for h in range(heads):
        prior = scores[h][:, :PL]
        recent = jnp.where(seen, scores[h][:, PL:], -1e30)
        top = jnp.max(jnp.maximum(prior, recent), -1, keepdims=True)
        prior = jnp.exp(prior - top)
        recent = jnp.exp(recent - top)
        inverse = 1.0 / jnp.sum(prior + recent, -1, keepdims=True)
        weights = jnp.concatenate(
            [(prior * inverse).astype(jnp.bfloat16), (recent * inverse).astype(jnp.bfloat16)], -1
        )
        mixed = jnp.dot(weights, values, preferred_element_type=jnp.float32)
        attn_ref[:, h * HD : (h + 1) * HD] = jnp.where(valid, mixed, 0.0).astype(jnp.bfloat16)


def attend(queries, keys, values, cache, valid, tokens):
    heads, rows, _ = queries.shape
    return pl.pallas_call(
        functools.partial(attend_kernel, tokens),
        in_specs=[VMEM] * 5,
        out_specs=VMEM,
        out_shape=jax.ShapeDtypeStruct((rows, heads * HD), jnp.bfloat16),
        compiler_params=params(8),
        cost_estimate=pl.CostEstimate(
            flops=8 * heads * rows * PL * HD,
            bytes_accessed=4 * rows * heads * HD,
            transcendentals=2 * heads * rows * PL,
        ),
    )(queries, keys, values, cache, valid)


def fetch_kernel(shift, after_ref, near_hbm, far_hbm, wo_ref, sems):
    del after_ref
    copies = out_weight_copies(0, shift, near_hbm, far_hbm, wo_ref, sems)
    for copy in copies:
        copy.start()
    for copy in copies:
        copy.wait()


def fetch(shift, after, out_near, out_far):
    depth, width = out_near.shape[0], out_near.shape[1] // (CHIPS * CORES)
    return pl.pallas_call(
        functools.partial(fetch_kernel, shift),
        in_specs=[ANY] * 3,
        out_specs=VMEM,
        out_shape=jax.ShapeDtypeStruct((1, 2 * depth, width), jnp.bfloat16),
        scratch_shapes=[pltpu.SemaphoreType.DMA((2, 1))],
        compiler_params=params(8),
        cost_estimate=pl.CostEstimate(
            flops=0, bytes_accessed=8 * depth * width, transcendentals=0
        ),
    )(after, in_hbm(out_near), in_hbm(out_far))


def output_cost(count, rows, depth, width):
    return pl.CostEstimate(
        flops=2 * count * rows * depth * width,
        bytes_accessed=2 * count * depth * width,
        transcendentals=0,
    )


def output_halves_kernel(near_ref, far_ref, wo_ref, top_ref, bottom_ref):
    half = top_ref.shape[0]
    both = jnp.concatenate([near_ref[...], far_ref[...]], -1)
    block = jnp.dot(both, wo_ref[0], preferred_element_type=jnp.float32).astype(jnp.bfloat16)
    top_ref[...] = block[:half]
    bottom_ref[...] = block[half:]


def output_halves(near, far, weights):
    rows = near.shape[0]
    _, depth, width = weights.shape
    return pl.pallas_call(
        output_halves_kernel,
        in_specs=[VMEM] * 3,
        out_specs=[VMEM] * 2,
        out_shape=[jax.ShapeDtypeStruct((rows // 2, width), jnp.bfloat16)] * 2,
        compiler_params=params(8),
        cost_estimate=output_cost(1, rows, depth, width),
    )(near, far, weights)


def output_kernel(shifts, near_ref, far_ref, near_hbm, far_hbm, *refs):
    outs, (wo_ref, sems) = refs[:-2], refs[-2:]
    copies = [
        out_weight_copies(i, shift, near_hbm, far_hbm, wo_ref, sems)
        for i, shift in enumerate(shifts)
    ]
    for pair in copies:
        for copy in pair:
            copy.start()
    both = jnp.concatenate([near_ref[...], far_ref[...]], -1)
    for i, out_ref in enumerate(outs):
        for copy in copies[i]:
            copy.wait()
        out_ref[...] = jnp.dot(both, wo_ref[i], preferred_element_type=jnp.float32)


def output(near, far, shifts, out_near, out_far):
    rows = near.shape[0]
    depth, width = out_near.shape[0], out_near.shape[1] // (CHIPS * CORES)
    return pl.pallas_call(
        functools.partial(output_kernel, shifts),
        in_specs=[VMEM] * 2 + [ANY] * 2,
        out_specs=[VMEM] * len(shifts),
        out_shape=[jax.ShapeDtypeStruct((rows, width), jnp.float32)] * len(shifts),
        scratch_shapes=[
            pltpu.VMEM((len(shifts), 2 * depth, width), jnp.bfloat16),
            pltpu.SemaphoreType.DMA((2, len(shifts))),
        ],
        compiler_params=params(8),
        cost_estimate=output_cost(len(shifts), rows, 2 * depth, width),
    )(near, far, in_hbm(out_near), in_hbm(out_far))


def pass_on_kernel(above_ref, below_ref, top_ref, bottom_ref, to_above_ref, to_below_ref):
    half = top_ref.shape[0]
    top = above_ref[:half] + top_ref[...].astype(jnp.float32)
    to_above_ref[:half] = top.astype(jnp.bfloat16)
    to_above_ref[half:] = above_ref[half:].astype(jnp.bfloat16)
    bottom = below_ref[half:] + bottom_ref[...].astype(jnp.float32)
    to_below_ref[:half] = below_ref[:half].astype(jnp.bfloat16)
    to_below_ref[half:] = bottom.astype(jnp.bfloat16)


def pass_on(above, below, top, bottom):
    block = jax.ShapeDtypeStruct(above.shape, jnp.bfloat16)
    return pl.pallas_call(
        pass_on_kernel,
        in_specs=[VMEM] * 4,
        out_specs=[VMEM] * 2,
        out_shape=[block, block],
        compiler_params=params(8),
    )(above, below, top, bottom)


def place_kernel(pick_ref, mine_ref, *refs):
    parts, out_ref = refs[:-1], refs[-1]
    total = mine_ref[...]
    for part in parts:
        total = total + part[...].astype(jnp.float32)
    placed = jnp.dot(
        pick_ref[...], total.astype(jnp.bfloat16), preferred_element_type=jnp.float32
    )
    out_ref[...] = placed.astype(jnp.bfloat16).reshape(out_ref.shape)


def place(pick, mine, parts, slots, tokens):
    _, width = mine.shape
    return pl.pallas_call(
        place_kernel,
        in_specs=[VMEM] * (2 + len(parts)),
        out_specs=VMEM,
        out_shape=jax.ShapeDtypeStruct((slots, tokens, width), jnp.bfloat16),
        compiler_params=params(8),
    )(pick, mine, *parts)


def block_picks(source, size, count):
    rows = source[:, None] * size + jnp.arange(size)[None, :]
    rows = jnp.where(source[:, None] >= 0, rows, -1).reshape(-1)
    return (rows[:, None] == jnp.arange(count * size)[None, :]).astype(jnp.bfloat16)


def per_device(resp_rows, resp_len, resp_shard, group_prompt, prompt_kv, w_query, w_keyval, w_out):
    learners = lax.axis_size("seq")
    group = lax.axis_index("seq")
    group_size, tokens, width = resp_rows.shape
    rows = group_size * tokens

    pieces = prompt_kv.reshape(learners, -1, HD)
    prompt_picks = block_picks(group_prompt, pieces.shape[1], learners)
    pieces = lax.all_to_all(pieces, "seq", 0, 0, tiled=True)

    x = resp_rows.reshape(rows, width)
    swap = lambda v: lax.ppermute(v, "tp", CORE_SWAP)
    below = lax.ppermute(x, "tp", chip_shift(1))
    above = lax.ppermute(x, "tp", chip_shift(-1))
    across = lax.ppermute(x, "tp", chip_shift(2))
    cache = lax.all_to_all(route(prompt_picks, pieces), "seq", 0, 0, tiled=True)
    out_far = swap(w_out)
    shards = [swap(x), below, swap(below), above, swap(above), across, swap(across)]

    own_len = lax.dynamic_slice_in_dim(resp_len, group * group_size, group_size, 0)
    valid = (jnp.arange(tokens)[None, :] < own_len[:, None]).astype(jnp.float32)
    valid = jnp.broadcast_to(valid.reshape(rows, 1), (rows, HD))
    cosine, sine = rope_tables(tokens, rows)
    own_shard = lax.dynamic_slice_in_dim(resp_shard[:, 0], group * group_size, group_size, 0)
    match = own_shard[None, :] == jnp.arange(learners)[:, None]
    pick = jnp.max(jnp.where(match, jnp.arange(group_size)[None, :], -1), -1)
    slot_picks = block_picks(pick, tokens, group_size)

    queries, keys, values = project(x, shards, w_query, w_keyval, cosine, sine)
    attn = attend(queries, keys, values, cache, valid, tokens)
    attn_far = swap(attn)
    w_across = fetch(2, attn, w_out, out_far)
    top, bottom = output_halves(attn, attn_far, w_across)
    top = lax.ppermute(top, "tp", chip_shift(1))
    bottom = lax.ppermute(bottom, "tp", chip_shift(-1))
    for_above, for_below = output(attn, attn_far, (1, -1), w_out, out_far)
    to_above, to_below = pass_on(for_above, for_below, top, bottom)
    (mine,) = output(attn, attn_far, (0,), w_out, out_far)
    parts = [
        lax.ppermute(to_above, "tp", chip_shift(1)),
        lax.ppermute(to_below, "tp", chip_shift(-1)),
    ]
    slots = place(slot_picks, mine, parts, learners, tokens)
    return lax.all_to_all(slots, "seq", 0, 0, tiled=True)


def solution(mesh):
    return jax.shard_map(
        per_device,
        mesh=mesh,
        in_specs=(
            P("seq", None, "tp"),
            P(),
            P(),
            P(),
            P(None, "seq", None, "tp"),
            P(None, "tp"),
            P(None, None, "tp"),
            P("tp", None),
        ),
        out_specs=P("seq", None, "tp"),
        check_vma=False,
    )
```

```python
import functools
import math

import jax
import jax.numpy as jnp
from jax import lax
from jax.experimental import pallas as pl
from jax.experimental.pallas import tpu as pltpu
from jax.sharding import PartitionSpec as P

HD = 128
PL = 256
ROPE_BASE = 1000000.0
CHIPS = 4
CORES = 2


def chip_shift(step):
    return [
        (y * CORES + c, ((y + step) % CHIPS) * CORES + c) for y in range(CHIPS) for c in range(CORES)
    ]


CORE_SWAP = [(i, i ^ 1) for i in range(CHIPS * CORES)]


def rope_tables(count):
    places = (PL + jnp.arange(count)).astype(jnp.float32)
    freqs = ROPE_BASE ** (-(jnp.arange(HD // 2).astype(jnp.float32) * 2.0 / HD))
    angles = places[:, None] * freqs[None, :]
    cosine, sine = jnp.cos(angles), jnp.sin(angles)
    return jnp.concatenate([cosine, cosine], -1), jnp.concatenate([-sine, sine], -1)


VMEM = pl.BlockSpec(memory_space=pltpu.VMEM)
SMEM = pl.BlockSpec(memory_space=pltpu.SMEM)
ANY = pl.BlockSpec(memory_space=pl.ANY)


def in_hbm(x):
    return pltpu.with_memory_space_constraint(x, pltpu.HBM)


def params(mib):
    return pltpu.CompilerParams(vmem_limit_bytes=mib * 1024 * 1024)


def place_in_column(shifts, far):
    me = lax.axis_index("tp")
    y, c = me // CORES, me % CORES
    core = 1 - c if far else c
    return [((y + shift + CHIPS) % CHIPS) * CORES + core for shift in shifts]


def columns_at(index, width):
    return pl.ds(pl.multiple_of(index * width, width), width)


def route_kernel(pick_ref, piece_ref, out_ref):
    count, size, width = piece_ref.shape
    pieces = piece_ref[...].reshape(count * size, width)
    picked = jnp.dot(pick_ref[...], pieces, preferred_element_type=jnp.float32)
    out_ref[...] = picked.astype(jnp.bfloat16).reshape(count, size, width)


def route(pick, pieces):
    return pl.pallas_call(
        route_kernel,
        in_specs=[VMEM, VMEM],
        out_specs=VMEM,
        out_shape=jax.ShapeDtypeStruct(pieces.shape, pieces.dtype),
        compiler_params=params(8),
    )(pick, pieces)


def weight_row_copies(i, index, wq_hbm, wkv_hbm, weights, sems):
    width = weights.shape[1]
    first = wq_hbm.shape[1]
    at = columns_at(index, width)
    return (
        pltpu.make_async_copy(wq_hbm.at[at, :], weights.at[i, :, 0:first], sems.at[0, i]),
        pltpu.make_async_copy(
            wkv_hbm.at[0, at, :], weights.at[i, :, first : first + HD], sems.at[1, i]
        ),
        pltpu.make_async_copy(
            wkv_hbm.at[1, at, :], weights.at[i, :, first + HD : first + 2 * HD], sems.at[2, i]
        ),
    )


def project_pairs(rows_ref, weights, copies, later):
    _, width, columns = weights.shape
    total = None
    for pair in range(len(copies) // 2):
        for copy in copies[2 * pair] + copies[2 * pair + 1]:
            copy.wait()
        if pair == 0:
            for group in later:
                for copy in group:
                    copy.start()
        part = jnp.dot(
            rows_ref[:, 2 * pair * width : 2 * (pair + 1) * width],
            weights[2 * pair : 2 * (pair + 1)].reshape(2 * width, columns),
            preferred_element_type=jnp.float32,
        )
        total = part if total is None else total + part
    return total


def out_weight_copies(i, shift, near_hbm, far_hbm, wo_ref, sems):
    depth = near_hbm.shape[0]
    at = columns_at(place_in_column((shift,), False)[0], wo_ref.shape[2])
    return (
        pltpu.make_async_copy(near_hbm.at[:, at], wo_ref.at[i, 0:depth, :], sems.at[0, i]),
        pltpu.make_async_copy(far_hbm.at[:, at], wo_ref.at[i, depth : 2 * depth, :], sems.at[1, i]),
    )


def project_kernel(*refs):
    shards = refs[:6]
    wq_hbm, wkv_hbm, acc_ref, last_ref, rows_ref, weights, sems, last_sems, row_sems = refs[6:]
    width = weights.shape[1]
    near = place_in_column((0, -1, 1, 2), False)
    far = place_in_column((0, -1, 1, 2), True)
    order = [index for pair in zip(near, far) for index in pair]
    copies = [
        (
            pltpu.make_async_copy(
                shard, rows_ref.at[:, i * width : (i + 1) * width], row_sems.at[i]
            ),
            *weight_row_copies(i, index, wq_hbm, wkv_hbm, weights, sems),
        )
        for i, (shard, index) in enumerate(zip(shards, order))
    ]
    last = [
        weight_row_copies(i, index, wq_hbm, wkv_hbm, last_ref, last_sems)
        for i, index in enumerate(order[6:])
    ]
    for group in copies[:4]:
        for copy in group:
            copy.start()
    acc_ref[...] = project_pairs(rows_ref, weights, copies, copies[4:] + last)
    for group in last:
        for copy in group:
            copy.wait()


def project(x, shards, w_query, w_keyval):
    rows, width = x.shape
    columns = w_query.shape[1] + 2 * HD
    return pl.pallas_call(
        project_kernel,
        in_specs=[ANY] * 8,
        out_specs=[VMEM] * 2,
        out_shape=[
            jax.ShapeDtypeStruct((rows, columns), jnp.float32),
            jax.ShapeDtypeStruct((2, width, columns), jnp.bfloat16),
        ],
        scratch_shapes=[
            pltpu.VMEM((rows, 6 * width), jnp.bfloat16),
            pltpu.VMEM((6, width, columns), jnp.bfloat16),
            pltpu.SemaphoreType.DMA((3, 6)),
            pltpu.SemaphoreType.DMA((3, 2)),
            pltpu.SemaphoreType.DMA((6,)),
        ],
        compiler_params=params(16),
        cost_estimate=pl.CostEstimate(
            flops=2 * rows * 6 * width * columns,
            bytes_accessed=16 * width * columns,
            transcendentals=0,
        ),
    )(*[in_hbm(v) for v in (x, *shards, w_query, w_keyval)])


def attend_kernel(
    tokens, acc_ref, near_ref, far_ref, weight_ref, cos_ref, sin_ref, cache_ref, valid_ref, attn_ref
):
    rows, columns = acc_ref.shape
    heads = columns // HD - 2
    width = near_ref.shape[1]
    shard = jnp.concatenate([near_ref[...], far_ref[...]], -1)
    both = acc_ref[...] + jnp.dot(
        shard, weight_ref[...].reshape(2 * width, columns), preferred_element_type=jnp.float32
    )
    cosine, sine = cos_ref[...][None], sin_ref[...][None]

    def rotated(h):
        v = both[:, h * HD : (h + 1) * HD]
        turned = pltpu.roll(v, HD // 2, 1).reshape(-1, tokens, HD) * sine
        return (v.reshape(-1, tokens, HD) * cosine + turned).astype(jnp.bfloat16).reshape(rows, HD)

    scale = 1.0 / math.sqrt(HD)
    half = cache_ref.shape[0] // 2
    own_values = both[:, (heads + 1) * HD :].astype(jnp.bfloat16)
    keys = jnp.concatenate([cache_ref[:half].reshape(PL, HD), rotated(heads)], 0)
    values = jnp.concatenate([cache_ref[half:].reshape(PL, HD), own_values], 0)
    row = lax.broadcasted_iota(jnp.int32, (rows, rows), 0)
    col = lax.broadcasted_iota(jnp.int32, (rows, rows), 1)
    seen = (row // tokens == col // tokens) & (col <= row)
    valid = valid_ref[...].astype(jnp.float32) > 0.0
    nt = (((1,), (1,)), ((), ()))
    scores = [
        lax.dot_general(rotated(h), keys, nt, preferred_element_type=jnp.float32) * scale
        for h in range(heads)
    ]
    for h in range(heads):
        prior = scores[h][:, :PL]
        recent = jnp.where(seen, scores[h][:, PL:], -1e30)
        top = jnp.max(jnp.maximum(prior, recent), -1, keepdims=True)
        prior = jnp.exp(prior - top)
        recent = jnp.exp(recent - top)
        inverse = 1.0 / jnp.sum(prior + recent, -1, keepdims=True)
        weights = jnp.concatenate(
            [(prior * inverse).astype(jnp.bfloat16), (recent * inverse).astype(jnp.bfloat16)], -1
        )
        mixed = jnp.dot(weights, values, preferred_element_type=jnp.float32)
        attn_ref[:, h * HD : (h + 1) * HD] = jnp.where(valid, mixed, 0.0).astype(jnp.bfloat16)


def attend(acc, near, far, weights, cosine, sine, cache, valid, tokens):
    rows, columns = acc.shape
    heads = columns // HD - 2
    return pl.pallas_call(
        functools.partial(attend_kernel, tokens),
        in_specs=[VMEM] * 8,
        out_specs=VMEM,
        out_shape=jax.ShapeDtypeStruct((rows, heads * HD), jnp.bfloat16),
        compiler_params=params(16),
        cost_estimate=pl.CostEstimate(
            flops=8 * heads * rows * PL * HD,
            bytes_accessed=4 * rows * heads * HD,
            transcendentals=2 * heads * rows * PL,
        ),
    )(acc, near, far, weights, cosine, sine, cache, valid)


def fetch_kernel(shift, after_ref, near_hbm, far_hbm, wo_ref, sems):
    del after_ref
    copies = out_weight_copies(0, shift, near_hbm, far_hbm, wo_ref, sems)
    for copy in copies:
        copy.start()
    for copy in copies:
        copy.wait()


def fetch(shift, after, out_near, out_far):
    depth, width = out_near.shape[0], out_near.shape[1] // (CHIPS * CORES)
    return pl.pallas_call(
        functools.partial(fetch_kernel, shift),
        in_specs=[ANY] * 3,
        out_specs=VMEM,
        out_shape=jax.ShapeDtypeStruct((1, 2 * depth, width), jnp.bfloat16),
        scratch_shapes=[pltpu.SemaphoreType.DMA((2, 1))],
        compiler_params=params(8),
        cost_estimate=pl.CostEstimate(
            flops=0, bytes_accessed=8 * depth * width, transcendentals=0
        ),
    )(after, in_hbm(out_near), in_hbm(out_far))


def output_cost(count, rows, depth, width):
    return pl.CostEstimate(
        flops=2 * count * rows * depth * width,
        bytes_accessed=2 * count * depth * width,
        transcendentals=0,
    )


def output_halves_kernel(near_ref, far_ref, wo_ref, top_ref, bottom_ref):
    half = top_ref.shape[0]
    both = jnp.concatenate([near_ref[...], far_ref[...]], -1)
    block = jnp.dot(both, wo_ref[0], preferred_element_type=jnp.float32).astype(jnp.bfloat16)
    top_ref[...] = block[:half]
    bottom_ref[...] = block[half:]


def output_halves(near, far, weights):
    rows = near.shape[0]
    _, depth, width = weights.shape
    return pl.pallas_call(
        output_halves_kernel,
        in_specs=[VMEM] * 3,
        out_specs=[VMEM] * 2,
        out_shape=[jax.ShapeDtypeStruct((rows // 2, width), jnp.bfloat16)] * 2,
        compiler_params=params(8),
        cost_estimate=output_cost(1, rows, depth, width),
    )(near, far, weights)


def output_kernel(shifts, near_ref, far_ref, near_hbm, far_hbm, *refs):
    outs, (wo_ref, sems) = refs[:-2], refs[-2:]
    copies = [
        out_weight_copies(i, shift, near_hbm, far_hbm, wo_ref, sems)
        for i, shift in enumerate(shifts)
    ]
    for pair in copies:
        for copy in pair:
            copy.start()
    both = jnp.concatenate([near_ref[...], far_ref[...]], -1)
    for i, out_ref in enumerate(outs):
        for copy in copies[i]:
            copy.wait()
        out_ref[...] = jnp.dot(both, wo_ref[i], preferred_element_type=jnp.float32)


def output(near, far, shifts, out_near, out_far):
    rows = near.shape[0]
    depth, width = out_near.shape[0], out_near.shape[1] // (CHIPS * CORES)
    return pl.pallas_call(
        functools.partial(output_kernel, shifts),
        in_specs=[VMEM] * 2 + [ANY] * 2,
        out_specs=[VMEM] * len(shifts),
        out_shape=[jax.ShapeDtypeStruct((rows, width), jnp.float32)] * len(shifts),
        scratch_shapes=[
            pltpu.VMEM((len(shifts), 2 * depth, width), jnp.bfloat16),
            pltpu.SemaphoreType.DMA((2, len(shifts))),
        ],
        compiler_params=params(8),
        cost_estimate=output_cost(len(shifts), rows, 2 * depth, width),
    )(near, far, in_hbm(out_near), in_hbm(out_far))


def pass_on_kernel(above_ref, below_ref, top_ref, bottom_ref, to_above_ref, to_below_ref):
    half = top_ref.shape[0]
    top = above_ref[:half] + top_ref[...].astype(jnp.float32)
    to_above_ref[:half] = top.astype(jnp.bfloat16)
    to_above_ref[half:] = above_ref[half:].astype(jnp.bfloat16)
    bottom = below_ref[half:] + bottom_ref[...].astype(jnp.float32)
    to_below_ref[:half] = below_ref[:half].astype(jnp.bfloat16)
    to_below_ref[half:] = bottom.astype(jnp.bfloat16)


def pass_on(above, below, top, bottom):
    block = jax.ShapeDtypeStruct(above.shape, jnp.bfloat16)
    return pl.pallas_call(
        pass_on_kernel,
        in_specs=[VMEM] * 4,
        out_specs=[VMEM] * 2,
        out_shape=[block, block],
        compiler_params=params(8),
    )(above, below, top, bottom)


def place_kernel(pick_ref, mine_ref, *refs):
    parts, out_ref = refs[:-1], refs[-1]
    total = mine_ref[...]
    for part in parts:
        total = total + part[...].astype(jnp.float32)
    slots, tokens, _ = out_ref.shape
    rows = total.shape[0]
    source = lax.broadcasted_iota(jnp.int32, (slots, rows), 1) // tokens
    row = lax.broadcasted_iota(jnp.int32, (slots, tokens, rows), 2) % tokens
    token = lax.broadcasted_iota(jnp.int32, (slots, tokens, rows), 1)
    chosen = jnp.where(source == pick_ref[...], 1.0, 0.0)[:, None, :]
    picks = jnp.where(row == token, chosen, 0.0).astype(jnp.bfloat16).reshape(-1, rows)
    placed = jnp.dot(picks, total.astype(jnp.bfloat16), preferred_element_type=jnp.float32)
    out_ref[...] = placed.astype(jnp.bfloat16).reshape(out_ref.shape)


def place(pick, mine, parts, slots, tokens):
    _, width = mine.shape
    return pl.pallas_call(
        place_kernel,
        in_specs=[VMEM] * (2 + len(parts)),
        out_specs=VMEM,
        out_shape=jax.ShapeDtypeStruct((slots, tokens, width), jnp.bfloat16),
        compiler_params=params(8),
    )(pick, mine, *parts)


def block_picks(source, size, count):
    rows = source[:, None] * size + jnp.arange(size)[None, :]
    rows = jnp.where(source[:, None] >= 0, rows, -1).reshape(-1)
    return (rows[:, None] == jnp.arange(count * size)[None, :]).astype(jnp.bfloat16)


def per_device(resp_rows, resp_len, resp_shard, group_prompt, prompt_kv, w_query, w_keyval, w_out):
    learners = lax.axis_size("seq")
    group = lax.axis_index("seq")
    group_size, tokens, width = resp_rows.shape
    rows = group_size * tokens

    pieces = prompt_kv.reshape(learners, -1, HD)
    prompt_picks = block_picks(group_prompt, pieces.shape[1], learners)
    pieces = lax.all_to_all(pieces, "seq", 0, 0, tiled=True)

    x = resp_rows.reshape(rows, width)
    swap = lambda v: lax.ppermute(v, "tp", CORE_SWAP)
    below = lax.ppermute(x, "tp", chip_shift(1))
    above = lax.ppermute(x, "tp", chip_shift(-1))
    x_again, below, above = lax.optimization_barrier((x, below, above))
    across = lax.ppermute(x_again, "tp", chip_shift(2))
    out_far = swap(w_out)
    shards = [swap(x), below, swap(below), above, swap(above)]
    pieces, *shards = lax.optimization_barrier((pieces, *shards))
    cache = lax.all_to_all(route(prompt_picks, pieces), "seq", 0, 0, tiled=True)

    own_len = lax.dynamic_slice_in_dim(resp_len, group * group_size, group_size, 0)
    valid = (jnp.arange(tokens)[None, :] < own_len[:, None]).astype(jnp.bfloat16)
    valid = jnp.broadcast_to(valid.reshape(rows, 1), (rows, HD))
    cosine, sine = rope_tables(tokens)
    own_shard = lax.dynamic_slice_in_dim(resp_shard[:, 0], group * group_size, group_size, 0)
    match = own_shard[None, :] == jnp.arange(learners)[:, None]
    pick = jnp.max(jnp.where(match, jnp.arange(group_size)[None, :], -1), -1)
    pick = jnp.broadcast_to(pick[:, None], (learners, rows)).astype(jnp.int32)

    acc, w_last = project(x, shards, w_query, w_keyval)
    attn = attend(acc, across, swap(across), w_last, cosine, sine, cache, valid, tokens)
    attn_far = swap(attn)
    w_across = fetch(2, attn, w_out, out_far)
    top, bottom = output_halves(attn, attn_far, w_across)
    top = lax.ppermute(top, "tp", chip_shift(1))
    bottom = lax.ppermute(bottom, "tp", chip_shift(-1))
    for_above, for_below = output(attn, attn_far, (1, -1), w_out, out_far)
    to_above, to_below = pass_on(for_above, for_below, top, bottom)
    (mine,) = output(attn, attn_far, (0,), w_out, out_far)
    parts = [
        lax.ppermute(to_above, "tp", chip_shift(1)),
        lax.ppermute(to_below, "tp", chip_shift(-1)),
    ]
    slots = place(pick, mine, parts, learners, tokens)
    return lax.all_to_all(slots, "seq", 0, 0, tiled=True)


def solution(mesh):
    return jax.shard_map(
        per_device,
        mesh=mesh,
        in_specs=(
            P("seq", None, "tp"),
            P(),
            P(),
            P(),
            P(None, "seq", None, "tp"),
            P(None, "tp"),
            P(None, None, "tp"),
            P("tp", None),
        ),
        out_specs=P("seq", None, "tp"),
        check_vma=False,
    )
```

```python
import functools
import math

import jax
import jax.numpy as jnp
from jax import lax
from jax.experimental import pallas as pl
from jax.experimental.pallas import tpu as pltpu
from jax.sharding import PartitionSpec as P

HD = 128
PL = 256
ROPE_BASE = 1000000.0
CHIPS = 4
CORES = 2


def chip_shift(step):
    return [
        (y * CORES + c, ((y + step) % CHIPS) * CORES + c) for y in range(CHIPS) for c in range(CORES)
    ]


CORE_SWAP = [(i, i ^ 1) for i in range(CHIPS * CORES)]


def rope_tables(count):
    places = (PL + jnp.arange(count)).astype(jnp.float32)
    freqs = ROPE_BASE ** (-(jnp.arange(HD // 2).astype(jnp.float32) * 2.0 / HD))
    angles = places[:, None] * freqs[None, :]
    cosine, sine = jnp.cos(angles), jnp.sin(angles)
    return jnp.concatenate([cosine, cosine], -1), jnp.concatenate([-sine, sine], -1)


VMEM = pl.BlockSpec(memory_space=pltpu.VMEM)
SMEM = pl.BlockSpec(memory_space=pltpu.SMEM)
ANY = pl.BlockSpec(memory_space=pl.ANY)


def in_hbm(x):
    return pltpu.with_memory_space_constraint(x, pltpu.HBM)


def params(mib):
    return pltpu.CompilerParams(vmem_limit_bytes=mib * 1024 * 1024)


def place_in_column(shifts, far):
    me = lax.axis_index("tp")
    y, c = me // CORES, me % CORES
    core = 1 - c if far else c
    return [((y + shift + CHIPS) % CHIPS) * CORES + core for shift in shifts]


def columns_at(index, width):
    return pl.ds(pl.multiple_of(index * width, width), width)


def block_picks(source, slots, size, rows):
    block = lax.broadcasted_iota(jnp.int32, (slots, rows), 1) // size
    row = lax.broadcasted_iota(jnp.int32, (slots, size, rows), 2) % size
    place = lax.broadcasted_iota(jnp.int32, (slots, size, rows), 1)
    chosen = jnp.where(block == source, 1.0, 0.0)[:, None, :]
    return jnp.where(row == place, chosen, 0.0).astype(jnp.bfloat16).reshape(-1, rows)


def route_kernel(pick_ref, piece_ref, out_ref):
    count, size, width = piece_ref.shape
    pieces = piece_ref[...].reshape(count * size, width)
    picked = jnp.dot(pick_ref[...], pieces, preferred_element_type=jnp.float32)
    out_ref[...] = picked.astype(jnp.bfloat16).reshape(count, size, width)


def route(pick, pieces):
    return pl.pallas_call(
        route_kernel,
        in_specs=[VMEM, VMEM],
        out_specs=VMEM,
        out_shape=jax.ShapeDtypeStruct(pieces.shape, pieces.dtype),
        compiler_params=params(8),
    )(pick, pieces)


def weight_row_copies(i, index, wq_hbm, wkv_hbm, weights, sems):
    width = weights.shape[1]
    first = wq_hbm.shape[1]
    at = columns_at(index, width)
    return (
        pltpu.make_async_copy(wq_hbm.at[at, :], weights.at[i, :, 0:first], sems.at[0, i]),
        pltpu.make_async_copy(
            wkv_hbm.at[0, at, :], weights.at[i, :, first : first + HD], sems.at[1, i]
        ),
        pltpu.make_async_copy(
            wkv_hbm.at[1, at, :], weights.at[i, :, first + HD : first + 2 * HD], sems.at[2, i]
        ),
    )


def project_pairs(rows_ref, weights, copies, later):
    _, width, columns = weights.shape
    total = None
    for pair in range(len(copies) // 2):
        for copy in copies[2 * pair] + copies[2 * pair + 1]:
            copy.wait()
        for group in later[pair] if pair < len(later) else ():
            for copy in group:
                copy.start()
        part = jnp.dot(
            rows_ref[:, 2 * pair * width : 2 * (pair + 1) * width],
            weights[2 * pair : 2 * (pair + 1)].reshape(2 * width, columns),
            preferred_element_type=jnp.float32,
        )
        total = part if total is None else total + part
    return total


def out_weight_copies(i, shift, near_hbm, far_hbm, wo_ref, sems):
    depth = near_hbm.shape[0]
    at = columns_at(place_in_column((shift,), False)[0], wo_ref.shape[2])
    return (
        pltpu.make_async_copy(near_hbm.at[:, at], wo_ref.at[i, 0:depth, :], sems.at[0, i]),
        pltpu.make_async_copy(far_hbm.at[:, at], wo_ref.at[i, depth : 2 * depth, :], sems.at[1, i]),
    )


def project_kernel(*refs):
    shards = refs[:6]
    wq_hbm, wkv_hbm, acc_ref, last_ref, rows_ref, weights, sems, last_sems, row_sems = refs[6:]
    width = weights.shape[1]
    near = place_in_column((0, -1, 1, 2), False)
    far = place_in_column((0, -1, 1, 2), True)
    order = [index for pair in zip(near, far) for index in pair]
    copies = [
        (
            pltpu.make_async_copy(
                shard, rows_ref.at[:, i * width : (i + 1) * width], row_sems.at[i]
            ),
            *weight_row_copies(i, index, wq_hbm, wkv_hbm, weights, sems),
        )
        for i, (shard, index) in enumerate(zip(shards, order))
    ]
    last = [
        weight_row_copies(i, index, wq_hbm, wkv_hbm, last_ref, last_sems)
        for i, index in enumerate(order[6:])
    ]
    for group in copies[:4]:
        for copy in group:
            copy.start()
    acc_ref[...] = project_pairs(rows_ref, weights, copies, [copies[4:], last])
    for group in last:
        for copy in group:
            copy.wait()


def project(x, shards, w_query, w_keyval):
    rows, width = x.shape
    columns = w_query.shape[1] + 2 * HD
    return pl.pallas_call(
        project_kernel,
        in_specs=[ANY] * 8,
        out_specs=[VMEM] * 2,
        out_shape=[
            jax.ShapeDtypeStruct((rows, columns), jnp.float32),
            jax.ShapeDtypeStruct((2, width, columns), jnp.bfloat16),
        ],
        scratch_shapes=[
            pltpu.VMEM((rows, 6 * width), jnp.bfloat16),
            pltpu.VMEM((6, width, columns), jnp.bfloat16),
            pltpu.SemaphoreType.DMA((3, 6)),
            pltpu.SemaphoreType.DMA((3, 2)),
            pltpu.SemaphoreType.DMA((6,)),
        ],
        compiler_params=params(16),
        cost_estimate=pl.CostEstimate(
            flops=2 * rows * 6 * width * columns,
            bytes_accessed=16 * width * columns,
            transcendentals=0,
        ),
    )(*[in_hbm(v) for v in (x, *shards, w_query, w_keyval)])


def attend_kernel(
    tokens, acc_ref, near_ref, far_ref, weight_ref, cos_ref, sin_ref, cache_ref, attn_ref
):
    rows, columns = acc_ref.shape
    heads = columns // HD - 2
    width = near_ref.shape[1]
    shard = jnp.concatenate([near_ref[...], far_ref[...]], -1)
    both = acc_ref[...] + jnp.dot(
        shard, weight_ref[...].reshape(2 * width, columns), preferred_element_type=jnp.float32
    )
    cosine, sine = cos_ref[...][None], sin_ref[...][None]

    def rotated(h):
        v = both[:, h * HD : (h + 1) * HD]
        turned = pltpu.roll(v, HD // 2, 1).reshape(-1, tokens, HD) * sine
        return (v.reshape(-1, tokens, HD) * cosine + turned).astype(jnp.bfloat16).reshape(rows, HD)

    scale = 1.0 / math.sqrt(HD)
    half = cache_ref.shape[0] // 2
    own_values = both[:, (heads + 1) * HD :].astype(jnp.bfloat16)
    keys = jnp.concatenate([cache_ref[:half].reshape(PL, HD), rotated(heads)], 0)
    values = jnp.concatenate([cache_ref[half:].reshape(PL, HD), own_values], 0)
    row = lax.broadcasted_iota(jnp.int32, (rows, rows), 0)
    col = lax.broadcasted_iota(jnp.int32, (rows, rows), 1)
    seen = (row // tokens == col // tokens) & (col <= row)
    nt = (((1,), (1,)), ((), ()))
    scores = [
        lax.dot_general(rotated(h), keys, nt, preferred_element_type=jnp.float32) * scale
        for h in range(heads)
    ]
    for h in range(heads):
        prior = scores[h][:, :PL]
        recent = jnp.where(seen, scores[h][:, PL:], -1e30)
        top = jnp.max(jnp.maximum(prior, recent), -1, keepdims=True)
        prior = jnp.exp(prior - top)
        recent = jnp.exp(recent - top)
        inverse = 1.0 / jnp.sum(prior + recent, -1, keepdims=True)
        weights = jnp.concatenate(
            [(prior * inverse).astype(jnp.bfloat16), (recent * inverse).astype(jnp.bfloat16)], -1
        )
        mixed = jnp.dot(weights, values, preferred_element_type=jnp.float32)
        attn_ref[:, h * HD : (h + 1) * HD] = mixed.astype(jnp.bfloat16)


def attend(acc, near, far, weights, cosine, sine, cache, tokens):
    rows, columns = acc.shape
    heads = columns // HD - 2
    return pl.pallas_call(
        functools.partial(attend_kernel, tokens),
        in_specs=[VMEM] * 7,
        out_specs=VMEM,
        out_shape=jax.ShapeDtypeStruct((rows, heads * HD), jnp.bfloat16),
        compiler_params=params(16),
        cost_estimate=pl.CostEstimate(
            flops=8 * heads * rows * PL * HD,
            bytes_accessed=4 * rows * heads * HD,
            transcendentals=2 * heads * rows * PL,
        ),
    )(acc, near, far, weights, cosine, sine, cache)


def fetch_kernel(shift, after_ref, near_hbm, far_hbm, wo_ref, sems):
    del after_ref
    copies = out_weight_copies(0, shift, near_hbm, far_hbm, wo_ref, sems)
    for copy in copies:
        copy.start()
    for copy in copies:
        copy.wait()


def fetch(shift, after, out_near, out_far):
    depth, width = out_near.shape[0], out_near.shape[1] // (CHIPS * CORES)
    return pl.pallas_call(
        functools.partial(fetch_kernel, shift),
        in_specs=[ANY] * 3,
        out_specs=VMEM,
        out_shape=jax.ShapeDtypeStruct((1, 2 * depth, width), jnp.bfloat16),
        scratch_shapes=[pltpu.SemaphoreType.DMA((2, 1))],
        compiler_params=params(8),
        cost_estimate=pl.CostEstimate(
            flops=0, bytes_accessed=8 * depth * width, transcendentals=0
        ),
    )(after, in_hbm(out_near), in_hbm(out_far))


def output_cost(count, rows, depth, width):
    return pl.CostEstimate(
        flops=2 * count * rows * depth * width,
        bytes_accessed=2 * count * depth * width,
        transcendentals=0,
    )


def output_halves_kernel(near_ref, far_ref, wo_ref, top_ref, bottom_ref):
    half = top_ref.shape[0]
    both = jnp.concatenate([near_ref[...], far_ref[...]], -1)
    block = jnp.dot(both, wo_ref[0], preferred_element_type=jnp.float32).astype(jnp.bfloat16)
    top_ref[...] = block[:half]
    bottom_ref[...] = block[half:]


def output_halves(near, far, weights):
    rows = near.shape[0]
    _, depth, width = weights.shape
    return pl.pallas_call(
        output_halves_kernel,
        in_specs=[VMEM] * 3,
        out_specs=[VMEM] * 2,
        out_shape=[jax.ShapeDtypeStruct((rows // 2, width), jnp.bfloat16)] * 2,
        compiler_params=params(8),
        cost_estimate=output_cost(1, rows, depth, width),
    )(near, far, weights)


def output_kernel(shifts, near_ref, far_ref, near_hbm, far_hbm, *refs):
    outs, (wo_ref, sems) = refs[:-2], refs[-2:]
    copies = [
        out_weight_copies(i, shift, near_hbm, far_hbm, wo_ref, sems)
        for i, shift in enumerate(shifts)
    ]
    for pair in copies:
        for copy in pair:
            copy.start()
    both = jnp.concatenate([near_ref[...], far_ref[...]], -1)
    for i, out_ref in enumerate(outs):
        for copy in copies[i]:
            copy.wait()
        out_ref[...] = jnp.dot(both, wo_ref[i], preferred_element_type=jnp.float32)


def output(near, far, shifts, out_near, out_far):
    rows = near.shape[0]
    depth, width = out_near.shape[0], out_near.shape[1] // (CHIPS * CORES)
    return pl.pallas_call(
        functools.partial(output_kernel, shifts),
        in_specs=[VMEM] * 2 + [ANY] * 2,
        out_specs=[VMEM] * len(shifts),
        out_shape=[jax.ShapeDtypeStruct((rows, width), jnp.float32)] * len(shifts),
        scratch_shapes=[
            pltpu.VMEM((len(shifts), 2 * depth, width), jnp.bfloat16),
            pltpu.SemaphoreType.DMA((2, len(shifts))),
        ],
        compiler_params=params(8),
        cost_estimate=output_cost(len(shifts), rows, 2 * depth, width),
    )(near, far, in_hbm(out_near), in_hbm(out_far))


def pass_on_kernel(above_ref, below_ref, top_ref, bottom_ref, to_above_ref, to_below_ref):
    half = top_ref.shape[0]
    top = above_ref[:half] + top_ref[...].astype(jnp.float32)
    to_above_ref[:half] = top.astype(jnp.bfloat16)
    to_above_ref[half:] = above_ref[half:].astype(jnp.bfloat16)
    bottom = below_ref[half:] + bottom_ref[...].astype(jnp.float32)
    to_below_ref[:half] = below_ref[:half].astype(jnp.bfloat16)
    to_below_ref[half:] = bottom.astype(jnp.bfloat16)


def pass_on(above, below, top, bottom):
    block = jax.ShapeDtypeStruct(above.shape, jnp.bfloat16)
    return pl.pallas_call(
        pass_on_kernel,
        in_specs=[VMEM] * 4,
        out_specs=[VMEM] * 2,
        out_shape=[block, block],
        compiler_params=params(8),
    )(above, below, top, bottom)


def place_kernel(pick_ref, count_ref, mine_ref, *refs):
    parts, out_ref = refs[:-1], refs[-1]
    total = mine_ref[...]
    for part in parts:
        total = total + part[...].astype(jnp.float32)
    slots, tokens, width = out_ref.shape
    picks = block_picks(pick_ref[...], slots, tokens, total.shape[0])
    placed = jnp.dot(picks, total.astype(jnp.bfloat16), preferred_element_type=jnp.float32)
    token = lax.broadcasted_iota(jnp.int32, (slots, tokens, width), 1)
    valid = token < count_ref[:, 0:1][:, None, :]
    out_ref[...] = jnp.where(valid, placed.reshape(slots, tokens, width), 0.0).astype(jnp.bfloat16)


def place(pick, count, mine, parts, slots, tokens):
    _, width = mine.shape
    return pl.pallas_call(
        place_kernel,
        in_specs=[VMEM] * (3 + len(parts)),
        out_specs=VMEM,
        out_shape=jax.ShapeDtypeStruct((slots, tokens, width), jnp.bfloat16),
        compiler_params=params(8),
    )(pick, count, mine, *parts)


def per_device(resp_rows, resp_len, resp_shard, group_prompt, prompt_kv, w_query, w_keyval, w_out):
    learners = lax.axis_size("seq")
    group = lax.axis_index("seq")
    group_size, tokens, width = resp_rows.shape
    rows = group_size * tokens

    pieces = prompt_kv.reshape(learners, -1, HD)
    size = pieces.shape[1]
    source = group_prompt[:, None] * size + jnp.arange(size)[None, :]
    prompts = (source.reshape(-1)[:, None] == jnp.arange(learners * size)[None, :]).astype(jnp.bfloat16)
    pieces = lax.all_to_all(pieces, "seq", 0, 0, tiled=True)

    x = resp_rows.reshape(rows, width)
    swap = lambda v: lax.ppermute(v, "tp", CORE_SWAP)
    below = lax.ppermute(x, "tp", chip_shift(1))
    above = lax.ppermute(x, "tp", chip_shift(-1))
    x_again, below, above = lax.optimization_barrier((x, below, above))
    x_far = swap(x_again)
    x_last, x_far = lax.optimization_barrier((x, x_far))
    across = lax.ppermute(x_last, "tp", chip_shift(2))
    out_far = swap(w_out)
    shards = [x_far, below, swap(below), above, swap(above)]
    pieces, *shards = lax.optimization_barrier((pieces, *shards))
    cache = lax.all_to_all(route(prompts, pieces), "seq", 0, 0, tiled=True)

    cosine, sine = rope_tables(tokens)
    acc, w_last = project(x, shards, w_query, w_keyval)
    attn = attend(acc, across, swap(across), w_last, cosine, sine, cache, tokens)
    resp_len, resp_shard, attn = lax.optimization_barrier((resp_len, resp_shard, attn))
    own_len = lax.dynamic_slice_in_dim(resp_len, group * group_size, group_size, 0)
    own_shard = lax.dynamic_slice_in_dim(resp_shard[:, 0], group * group_size, group_size, 0)
    match = own_shard[None, :] == jnp.arange(learners)[:, None]
    pick = jnp.max(jnp.where(match, jnp.arange(group_size)[None, :], -1), -1)
    count = jnp.max(jnp.where(match, own_len[None, :], 0), -1)
    spread = lambda v: jnp.broadcast_to(v[:, None], (learners, rows)).astype(jnp.int32)
    attn_far = swap(attn)
    w_across = fetch(2, attn, w_out, out_far)
    top, bottom = output_halves(attn, attn_far, w_across)
    top = lax.ppermute(top, "tp", chip_shift(1))
    bottom = lax.ppermute(bottom, "tp", chip_shift(-1))
    for_above, for_below = output(attn, attn_far, (1, -1), w_out, out_far)
    to_above, to_below = pass_on(for_above, for_below, top, bottom)
    (mine,) = output(attn, attn_far, (0,), w_out, out_far)
    parts = [
        lax.ppermute(to_above, "tp", chip_shift(1)),
        lax.ppermute(to_below, "tp", chip_shift(-1)),
    ]
    slots = place(spread(pick), spread(count), mine, parts, learners, tokens)
    return lax.all_to_all(slots, "seq", 0, 0, tiled=True)


def solution(mesh):
    return jax.shard_map(
        per_device,
        mesh=mesh,
        in_specs=(
            P("seq", None, "tp"),
            P(),
            P(),
            P(),
            P(None, "seq", None, "tp"),
            P(None, "tp"),
            P(None, None, "tp"),
            P("tp", None),
        ),
        out_specs=P("seq", None, "tp"),
        check_vma=False,
    )
```

```python
import functools
import math

import jax
import jax.numpy as jnp
from jax import lax
from jax.experimental import pallas as pl
from jax.experimental.pallas import tpu as pltpu
from jax.sharding import PartitionSpec as P

HD = 128
PL = 256
ROPE_BASE = 1000000.0
CHIPS = 4
CORES = 2


def chip_shift(step):
    return [
        (y * CORES + c, ((y + step) % CHIPS) * CORES + c) for y in range(CHIPS) for c in range(CORES)
    ]


CORE_SWAP = [(i, i ^ 1) for i in range(CHIPS * CORES)]


def rope_tables(count):
    places = (PL + jnp.arange(count)).astype(jnp.float32)
    freqs = ROPE_BASE ** (-(jnp.arange(HD // 2).astype(jnp.float32) * 2.0 / HD))
    angles = places[:, None] * freqs[None, :]
    cosine, sine = jnp.cos(angles), jnp.sin(angles)
    return jnp.concatenate([cosine, cosine], -1), jnp.concatenate([-sine, sine], -1)


VMEM = pl.BlockSpec(memory_space=pltpu.VMEM)
SMEM = pl.BlockSpec(memory_space=pltpu.SMEM)
ANY = pl.BlockSpec(memory_space=pl.ANY)


def in_hbm(x):
    return pltpu.with_memory_space_constraint(x, pltpu.HBM)


def params(mib):
    return pltpu.CompilerParams(vmem_limit_bytes=mib * 1024 * 1024)


def place_in_column(shifts, far):
    me = lax.axis_index("tp")
    y, c = me // CORES, me % CORES
    core = 1 - c if far else c
    return [((y + shift + CHIPS) % CHIPS) * CORES + core for shift in shifts]


def columns_at(index, width):
    return pl.ds(pl.multiple_of(index * width, width), width)


def block_picks(source, slots, size, rows):
    block = lax.broadcasted_iota(jnp.int32, (slots, rows), 1) // size
    row = lax.broadcasted_iota(jnp.int32, (slots, size, rows), 2) % size
    place = lax.broadcasted_iota(jnp.int32, (slots, size, rows), 1)
    chosen = jnp.where(block == source, 1.0, 0.0)[:, None, :]
    return jnp.where(row == place, chosen, 0.0).astype(jnp.bfloat16).reshape(-1, rows)


def route_kernel(pick_ref, piece_ref, out_ref):
    count, size, width = piece_ref.shape
    slots = out_ref.shape[0]
    part = pick_ref.shape[0] // slots
    for i in range(size // part):
        at = slice(i * part, (i + 1) * part)
        pieces = piece_ref[:, at, :].reshape(count * part, width)
        picked = jnp.dot(pick_ref[...], pieces, preferred_element_type=jnp.float32)
        out_ref[:, at, :] = picked.astype(jnp.bfloat16).reshape(slots, part, width)


def route(pick, pieces, slots):
    _, size, width = pieces.shape
    return pl.pallas_call(
        route_kernel,
        in_specs=[VMEM, VMEM],
        out_specs=VMEM,
        out_shape=jax.ShapeDtypeStruct((slots, size, width), pieces.dtype),
        compiler_params=params(8),
    )(pick, pieces)


def weight_row_copies(i, index, wq_hbm, wkv_hbm, weights, sems):
    width = weights.shape[1]
    first = wq_hbm.shape[1]
    at = columns_at(index, width)
    return (
        pltpu.make_async_copy(wq_hbm.at[at, :], weights.at[i, :, 0:first], sems.at[0, i]),
        pltpu.make_async_copy(
            wkv_hbm.at[0, at, :], weights.at[i, :, first : first + HD], sems.at[1, i]
        ),
        pltpu.make_async_copy(
            wkv_hbm.at[1, at, :], weights.at[i, :, first + HD : first + 2 * HD], sems.at[2, i]
        ),
    )


def project_pairs(rows_ref, weights, copies, later):
    _, width, columns = weights.shape
    total = None
    for pair in range(len(copies) // 2):
        for copy in copies[2 * pair] + copies[2 * pair + 1]:
            copy.wait()
        for group in later[pair] if pair < len(later) else ():
            for copy in group:
                copy.start()
        part = jnp.dot(
            rows_ref[:, 2 * pair * width : 2 * (pair + 1) * width],
            weights[2 * pair : 2 * (pair + 1)].reshape(2 * width, columns),
            preferred_element_type=jnp.float32,
        )
        total = part if total is None else total + part
    return total


def out_weight_copies(i, shift, near_hbm, far_hbm, wo_ref, sems):
    depth = near_hbm.shape[0]
    at = columns_at(place_in_column((shift,), False)[0], wo_ref.shape[2])
    return (
        pltpu.make_async_copy(near_hbm.at[:, at], wo_ref.at[i, 0:depth, :], sems.at[0, i]),
        pltpu.make_async_copy(far_hbm.at[:, at], wo_ref.at[i, depth : 2 * depth, :], sems.at[1, i]),
    )


def project_kernel(*refs):
    shards = refs[:6]
    wq_hbm, wkv_hbm, acc_ref, last_ref, rows_ref, weights, sems, last_sems, row_sems = refs[6:]
    width = weights.shape[1]
    near = place_in_column((0, -1, 1, 2), False)
    far = place_in_column((0, -1, 1, 2), True)
    order = [index for pair in zip(near, far) for index in pair]
    copies = [
        (
            pltpu.make_async_copy(
                shard, rows_ref.at[:, i * width : (i + 1) * width], row_sems.at[i]
            ),
            *weight_row_copies(i, index, wq_hbm, wkv_hbm, weights, sems),
        )
        for i, (shard, index) in enumerate(zip(shards, order))
    ]
    last = [
        weight_row_copies(i, index, wq_hbm, wkv_hbm, last_ref, last_sems)
        for i, index in enumerate(order[6:])
    ]
    for group in copies[:4]:
        for copy in group:
            copy.start()
    acc_ref[...] = project_pairs(rows_ref, weights, copies, [copies[4:], last])
    for group in last:
        for copy in group:
            copy.wait()


def project(x, shards, w_query, w_keyval):
    rows, width = x.shape
    columns = w_query.shape[1] + 2 * HD
    return pl.pallas_call(
        project_kernel,
        in_specs=[ANY] * 8,
        out_specs=[VMEM] * 2,
        out_shape=[
            jax.ShapeDtypeStruct((rows, columns), jnp.float32),
            jax.ShapeDtypeStruct((2, width, columns), jnp.bfloat16),
        ],
        scratch_shapes=[
            pltpu.VMEM((rows, 6 * width), jnp.bfloat16),
            pltpu.VMEM((6, width, columns), jnp.bfloat16),
            pltpu.SemaphoreType.DMA((3, 6)),
            pltpu.SemaphoreType.DMA((3, 2)),
            pltpu.SemaphoreType.DMA((6,)),
        ],
        compiler_params=params(16),
        cost_estimate=pl.CostEstimate(
            flops=2 * rows * 6 * width * columns,
            bytes_accessed=16 * width * columns,
            transcendentals=0,
        ),
    )(*[in_hbm(v) for v in (x, *shards, w_query, w_keyval)])


def attend_kernel(
    tokens, acc_ref, near_ref, far_ref, weight_ref, cos_ref, sin_ref, cache_ref, attn_ref
):
    rows, columns = acc_ref.shape
    heads = columns // HD - 2
    width = near_ref.shape[1]
    shard = jnp.concatenate([near_ref[...], far_ref[...]], -1)
    both = acc_ref[...] + jnp.dot(
        shard, weight_ref[...].reshape(2 * width, columns), preferred_element_type=jnp.float32
    )
    cosine, sine = cos_ref[...][None], sin_ref[...][None]

    def rotated(h):
        v = both[:, h * HD : (h + 1) * HD]
        turned = pltpu.roll(v, HD // 2, 1).reshape(-1, tokens, HD) * sine
        return (v.reshape(-1, tokens, HD) * cosine + turned).astype(jnp.bfloat16).reshape(rows, HD)

    scale = 1.0 / math.sqrt(HD)
    near = cache_ref.shape[0] // 2
    cache = cache_ref[:near] + cache_ref[near:]
    half = near // 2
    own_values = both[:, (heads + 1) * HD :].astype(jnp.bfloat16)
    keys = jnp.concatenate([cache[:half].reshape(PL, HD), rotated(heads)], 0)
    values = jnp.concatenate([cache[half:].reshape(PL, HD), own_values], 0)
    row = lax.broadcasted_iota(jnp.int32, (rows, rows), 0)
    col = lax.broadcasted_iota(jnp.int32, (rows, rows), 1)
    seen = (row // tokens == col // tokens) & (col <= row)
    nt = (((1,), (1,)), ((), ()))
    scores = [
        lax.dot_general(rotated(h), keys, nt, preferred_element_type=jnp.float32) * scale
        for h in range(heads)
    ]
    for h in range(heads):
        prior = scores[h][:, :PL]
        recent = jnp.where(seen, scores[h][:, PL:], -1e30)
        top = jnp.max(jnp.maximum(prior, recent), -1, keepdims=True)
        prior = jnp.exp(prior - top)
        recent = jnp.exp(recent - top)
        inverse = 1.0 / jnp.sum(prior + recent, -1, keepdims=True)
        weights = jnp.concatenate(
            [(prior * inverse).astype(jnp.bfloat16), (recent * inverse).astype(jnp.bfloat16)], -1
        )
        mixed = jnp.dot(weights, values, preferred_element_type=jnp.float32)
        attn_ref[:, h * HD : (h + 1) * HD] = mixed.astype(jnp.bfloat16)


def attend(acc, near, far, weights, cosine, sine, cache, tokens):
    rows, columns = acc.shape
    heads = columns // HD - 2
    return pl.pallas_call(
        functools.partial(attend_kernel, tokens),
        in_specs=[VMEM] * 7,
        out_specs=VMEM,
        out_shape=jax.ShapeDtypeStruct((rows, heads * HD), jnp.bfloat16),
        compiler_params=params(16),
        cost_estimate=pl.CostEstimate(
            flops=8 * heads * rows * PL * HD,
            bytes_accessed=4 * rows * heads * HD,
            transcendentals=2 * heads * rows * PL,
        ),
    )(acc, near, far, weights, cosine, sine, cache)


def fetch_kernel(shift, after_ref, near_hbm, far_hbm, wo_ref, sems):
    del after_ref
    copies = out_weight_copies(0, shift, near_hbm, far_hbm, wo_ref, sems)
    for copy in copies:
        copy.start()
    for copy in copies:
        copy.wait()


def fetch(shift, after, out_near, out_far):
    depth, width = out_near.shape[0], out_near.shape[1] // (CHIPS * CORES)
    return pl.pallas_call(
        functools.partial(fetch_kernel, shift),
        in_specs=[ANY] * 3,
        out_specs=VMEM,
        out_shape=jax.ShapeDtypeStruct((1, 2 * depth, width), jnp.bfloat16),
        scratch_shapes=[pltpu.SemaphoreType.DMA((2, 1))],
        compiler_params=params(8),
        cost_estimate=pl.CostEstimate(
            flops=0, bytes_accessed=8 * depth * width, transcendentals=0
        ),
    )(after, in_hbm(out_near), in_hbm(out_far))


def output_cost(count, rows, depth, width):
    return pl.CostEstimate(
        flops=2 * count * rows * depth * width,
        bytes_accessed=2 * count * depth * width,
        transcendentals=0,
    )


def output_halves_kernel(near_ref, far_ref, wo_ref, top_ref, bottom_ref):
    half = top_ref.shape[0]
    both = jnp.concatenate([near_ref[...], far_ref[...]], -1)
    block = jnp.dot(both, wo_ref[0], preferred_element_type=jnp.float32).astype(jnp.bfloat16)
    top_ref[...] = block[:half]
    bottom_ref[...] = block[half:]


def output_halves(near, far, weights):
    rows = near.shape[0]
    _, depth, width = weights.shape
    return pl.pallas_call(
        output_halves_kernel,
        in_specs=[VMEM] * 3,
        out_specs=[VMEM] * 2,
        out_shape=[jax.ShapeDtypeStruct((rows // 2, width), jnp.bfloat16)] * 2,
        compiler_params=params(8),
        cost_estimate=output_cost(1, rows, depth, width),
    )(near, far, weights)


def output_kernel(shifts, near_ref, far_ref, near_hbm, far_hbm, *refs):
    outs, (wo_ref, sems) = refs[:-2], refs[-2:]
    copies = [
        out_weight_copies(i, shift, near_hbm, far_hbm, wo_ref, sems)
        for i, shift in enumerate(shifts)
    ]
    for pair in copies:
        for copy in pair:
            copy.start()
    both = jnp.concatenate([near_ref[...], far_ref[...]], -1)
    for i, out_ref in enumerate(outs):
        for copy in copies[i]:
            copy.wait()
        out_ref[...] = jnp.dot(both, wo_ref[i], preferred_element_type=jnp.float32)


def output(near, far, shifts, out_near, out_far):
    rows = near.shape[0]
    depth, width = out_near.shape[0], out_near.shape[1] // (CHIPS * CORES)
    return pl.pallas_call(
        functools.partial(output_kernel, shifts),
        in_specs=[VMEM] * 2 + [ANY] * 2,
        out_specs=[VMEM] * len(shifts),
        out_shape=[jax.ShapeDtypeStruct((rows, width), jnp.float32)] * len(shifts),
        scratch_shapes=[
            pltpu.VMEM((len(shifts), 2 * depth, width), jnp.bfloat16),
            pltpu.SemaphoreType.DMA((2, len(shifts))),
        ],
        compiler_params=params(8),
        cost_estimate=output_cost(len(shifts), rows, 2 * depth, width),
    )(near, far, in_hbm(out_near), in_hbm(out_far))


def pass_on_kernel(above_ref, below_ref, top_ref, bottom_ref, to_above_ref, to_below_ref):
    half = top_ref.shape[0]
    top = above_ref[:half] + top_ref[...].astype(jnp.float32)
    to_above_ref[:half] = top.astype(jnp.bfloat16)
    to_above_ref[half:] = above_ref[half:].astype(jnp.bfloat16)
    bottom = below_ref[half:] + bottom_ref[...].astype(jnp.float32)
    to_below_ref[:half] = below_ref[:half].astype(jnp.bfloat16)
    to_below_ref[half:] = bottom.astype(jnp.bfloat16)


def pass_on(above, below, top, bottom):
    block = jax.ShapeDtypeStruct(above.shape, jnp.bfloat16)
    return pl.pallas_call(
        pass_on_kernel,
        in_specs=[VMEM] * 4,
        out_specs=[VMEM] * 2,
        out_shape=[block, block],
        compiler_params=params(8),
    )(above, below, top, bottom)


def place_kernel(pick_ref, count_ref, mine_ref, *refs):
    parts, out_ref = refs[:-1], refs[-1]
    total = mine_ref[...]
    for part in parts:
        total = total + part[...].astype(jnp.float32)
    slots, tokens, width = out_ref.shape
    picks = block_picks(pick_ref[...], slots, tokens, total.shape[0])
    placed = jnp.dot(picks, total.astype(jnp.bfloat16), preferred_element_type=jnp.float32)
    token = lax.broadcasted_iota(jnp.int32, (slots, tokens, width), 1)
    valid = token < count_ref[:, 0:1][:, None, :]
    out_ref[...] = jnp.where(valid, placed.reshape(slots, tokens, width), 0.0).astype(jnp.bfloat16)


def place(pick, count, mine, parts, slots, tokens):
    _, width = mine.shape
    return pl.pallas_call(
        place_kernel,
        in_specs=[VMEM] * (3 + len(parts)),
        out_specs=VMEM,
        out_shape=jax.ShapeDtypeStruct((slots, tokens, width), jnp.bfloat16),
        compiler_params=params(8),
    )(pick, count, mine, *parts)


def per_device(resp_rows, resp_len, resp_shard, group_prompt, prompt_kv, w_query, w_keyval, w_out):
    learners = lax.axis_size("seq")
    group = lax.axis_index("seq")
    group_size, tokens, width = resp_rows.shape
    rows = group_size * tokens

    near = learners // 2
    halves = [list(range(near)), list(range(near, learners))]
    pieces = prompt_kv.reshape(near, -1, HD)
    part = 16
    source = group_prompt - group // near * near
    held = (source >= 0) & (source < near)
    source = jnp.where(held, source, -near)[:, None] * part + jnp.arange(part)[None, :]
    prompts = source.reshape(-1)[:, None] == jnp.arange(near * part)[None, :]
    prompts = prompts.astype(jnp.bfloat16)
    pieces = lax.all_to_all(pieces, "seq", 0, 0, axis_index_groups=halves, tiled=True)

    x = resp_rows.reshape(rows, width)
    swap = lambda v: lax.ppermute(v, "tp", CORE_SWAP)
    below = lax.ppermute(x, "tp", chip_shift(1))
    above = lax.ppermute(x, "tp", chip_shift(-1))
    x_far = swap(x)
    x_last, below, above = lax.optimization_barrier((x, below, above))
    across = lax.ppermute(x_last, "tp", chip_shift(2))
    out_far = swap(w_out)
    shards = [x_far, below, swap(below), above, swap(above)]
    pieces, *shards = lax.optimization_barrier((pieces, *shards))
    cache = lax.all_to_all(route(prompts, pieces, learners), "seq", 0, 0, tiled=True)

    cosine, sine = rope_tables(tokens)
    acc, w_last = project(x, shards, w_query, w_keyval)
    attn = attend(acc, across, swap(across), w_last, cosine, sine, cache, tokens)
    resp_len, resp_shard, attn = lax.optimization_barrier((resp_len, resp_shard, attn))
    own_len = lax.dynamic_slice_in_dim(resp_len, group * group_size, group_size, 0)
    own_shard = lax.dynamic_slice_in_dim(resp_shard[:, 0], group * group_size, group_size, 0)
    match = own_shard[None, :] == jnp.arange(learners)[:, None]
    pick = jnp.max(jnp.where(match, jnp.arange(group_size)[None, :], -1), -1)
    count = jnp.max(jnp.where(match, own_len[None, :], 0), -1)
    spread = lambda v: jnp.broadcast_to(v[:, None], (learners, rows)).astype(jnp.int32)
    attn_far = swap(attn)
    w_across = fetch(2, attn, w_out, out_far)
    top, bottom = output_halves(attn, attn_far, w_across)
    top = lax.ppermute(top, "tp", chip_shift(1))
    bottom = lax.ppermute(bottom, "tp", chip_shift(-1))
    for_above, for_below = output(attn, attn_far, (1, -1), w_out, out_far)
    to_above, to_below = pass_on(for_above, for_below, top, bottom)
    (mine,) = output(attn, attn_far, (0,), w_out, out_far)
    parts = [
        lax.ppermute(to_above, "tp", chip_shift(1)),
        lax.ppermute(to_below, "tp", chip_shift(-1)),
    ]
    slots = place(spread(pick), spread(count), mine, parts, learners, tokens)
    return lax.all_to_all(slots, "seq", 0, 0, tiled=True)


def solution(mesh):
    return jax.shard_map(
        per_device,
        mesh=mesh,
        in_specs=(
            P("seq", None, "tp"),
            P(),
            P(),
            P(),
            P(None, "seq", None, "tp"),
            P(None, "tp"),
            P(None, None, "tp"),
            P("tp", None),
        ),
        out_specs=P("seq", None, "tp"),
        check_vma=False,
    )
```

```python
import functools
import math

import jax
import jax.numpy as jnp
from jax import lax
from jax.experimental import pallas as pl
from jax.experimental.pallas import tpu as pltpu
from jax.sharding import PartitionSpec as P

HD = 128
PL = 256
ROPE_BASE = 1000000.0
CHIPS = 4
CORES = 2


def chip_shift(step):
    return [
        (y * CORES + c, ((y + step) % CHIPS) * CORES + c) for y in range(CHIPS) for c in range(CORES)
    ]


CORE_SWAP = [(i, i ^ 1) for i in range(CHIPS * CORES)]


def rope_tables(count):
    places = (PL + jnp.arange(count)).astype(jnp.float32)
    freqs = ROPE_BASE ** (-(jnp.arange(HD // 2).astype(jnp.float32) * 2.0 / HD))
    angles = places[:, None] * freqs[None, :]
    cosine, sine = jnp.cos(angles), jnp.sin(angles)
    return jnp.concatenate([cosine, cosine], -1), jnp.concatenate([-sine, sine], -1)


VMEM = pl.BlockSpec(memory_space=pltpu.VMEM)
SMEM = pl.BlockSpec(memory_space=pltpu.SMEM)
ANY = pl.BlockSpec(memory_space=pl.ANY)


def in_hbm(x):
    return pltpu.with_memory_space_constraint(x, pltpu.HBM)


def params(mib):
    return pltpu.CompilerParams(vmem_limit_bytes=mib * 1024 * 1024)


def place_in_column(shifts, far):
    me = lax.axis_index("tp")
    y, c = me // CORES, me % CORES
    core = 1 - c if far else c
    return [((y + shift + CHIPS) % CHIPS) * CORES + core for shift in shifts]


def columns_at(index, width):
    return pl.ds(pl.multiple_of(index * width, width), width)


def block_picks(source, slots, size, rows):
    block = lax.broadcasted_iota(jnp.int32, (slots, rows), 1) // size
    row = lax.broadcasted_iota(jnp.int32, (slots, size, rows), 2) % size
    place = lax.broadcasted_iota(jnp.int32, (slots, size, rows), 1)
    chosen = jnp.where(block == source, 1.0, 0.0)[:, None, :]
    return jnp.where(row == place, chosen, 0.0).astype(jnp.bfloat16).reshape(-1, rows)


def route_kernel(pick_ref, piece_ref, out_ref):
    count, size, width = piece_ref.shape
    slots = out_ref.shape[0]
    part = pick_ref.shape[0] // slots
    for i in range(size // part):
        at = slice(i * part, (i + 1) * part)
        pieces = piece_ref[:, at, :].reshape(count * part, width)
        picked = jnp.dot(pick_ref[...], pieces, preferred_element_type=jnp.float32)
        out_ref[:, at, :] = picked.astype(jnp.bfloat16).reshape(slots, part, width)


def route(pick, pieces, slots):
    _, size, width = pieces.shape
    return pl.pallas_call(
        route_kernel,
        in_specs=[VMEM, VMEM],
        out_specs=VMEM,
        out_shape=jax.ShapeDtypeStruct((slots, size, width), pieces.dtype),
        compiler_params=params(8),
    )(pick, pieces)


def weight_row_copies(i, index, wq_hbm, wkv_hbm, weights, sems):
    width = weights.shape[1]
    first = wq_hbm.shape[1]
    at = columns_at(index, width)
    return (
        pltpu.make_async_copy(wq_hbm.at[at, :], weights.at[i, :, 0:first], sems.at[0, i]),
        pltpu.make_async_copy(
            wkv_hbm.at[0, at, :], weights.at[i, :, first : first + HD], sems.at[1, i]
        ),
        pltpu.make_async_copy(
            wkv_hbm.at[1, at, :], weights.at[i, :, first + HD : first + 2 * HD], sems.at[2, i]
        ),
    )


def project_pairs(rows_ref, weights, copies, later):
    _, width, columns = weights.shape
    total = None
    for pair in range(len(copies) // 2):
        for copy in copies[2 * pair] + copies[2 * pair + 1]:
            copy.wait()
        for group in later[pair] if pair < len(later) else ():
            for copy in group:
                copy.start()
        part = jnp.dot(
            rows_ref[:, 2 * pair * width : 2 * (pair + 1) * width],
            weights[2 * pair : 2 * (pair + 1)].reshape(2 * width, columns),
            preferred_element_type=jnp.float32,
        )
        total = part if total is None else total + part
    return total


def out_weight_copies(i, shift, near_hbm, far_hbm, wo_ref, sems):
    depth = near_hbm.shape[0]
    at = columns_at(place_in_column((shift,), False)[0], wo_ref.shape[2])
    return (
        pltpu.make_async_copy(near_hbm.at[:, at], wo_ref.at[i, 0:depth, :], sems.at[0, i]),
        pltpu.make_async_copy(far_hbm.at[:, at], wo_ref.at[i, depth : 2 * depth, :], sems.at[1, i]),
    )


def project_kernel(*refs):
    shards = refs[:6]
    wq_hbm, wkv_hbm, acc_ref, last_ref, rows_ref, weights, sems, last_sems, row_sems = refs[6:]
    width = weights.shape[1]
    near = place_in_column((0, -1, 1, 2), False)
    far = place_in_column((0, -1, 1, 2), True)
    order = [index for pair in zip(near, far) for index in pair]
    copies = [
        (
            pltpu.make_async_copy(
                shard, rows_ref.at[:, i * width : (i + 1) * width], row_sems.at[i]
            ),
            *weight_row_copies(i, index, wq_hbm, wkv_hbm, weights, sems),
        )
        for i, (shard, index) in enumerate(zip(shards, order))
    ]
    last = [
        weight_row_copies(i, index, wq_hbm, wkv_hbm, last_ref, last_sems)
        for i, index in enumerate(order[6:])
    ]
    for group in copies[:4]:
        for copy in group:
            copy.start()
    acc_ref[...] = project_pairs(rows_ref, weights, copies, [copies[4:], last])
    for group in last:
        for copy in group:
            copy.wait()


def project(x, shards, w_query, w_keyval):
    rows, width = x.shape
    columns = w_query.shape[1] + 2 * HD
    return pl.pallas_call(
        project_kernel,
        in_specs=[ANY] * 8,
        out_specs=[VMEM] * 2,
        out_shape=[
            jax.ShapeDtypeStruct((rows, columns), jnp.float32),
            jax.ShapeDtypeStruct((2, width, columns), jnp.bfloat16),
        ],
        scratch_shapes=[
            pltpu.VMEM((rows, 6 * width), jnp.bfloat16),
            pltpu.VMEM((6, width, columns), jnp.bfloat16),
            pltpu.SemaphoreType.DMA((3, 6)),
            pltpu.SemaphoreType.DMA((3, 2)),
            pltpu.SemaphoreType.DMA((6,)),
        ],
        compiler_params=params(16),
        cost_estimate=pl.CostEstimate(
            flops=2 * rows * 6 * width * columns,
            bytes_accessed=16 * width * columns,
            transcendentals=0,
        ),
    )(*[in_hbm(v) for v in (x, *shards, w_query, w_keyval)])


def attend_kernel(
    tokens, acc_ref, near_ref, far_ref, weight_ref, cos_ref, sin_ref, cache_ref, attn_ref
):
    rows, columns = acc_ref.shape
    heads = columns // HD - 2
    width = near_ref.shape[1]
    shard = jnp.concatenate([near_ref[...], far_ref[...]], -1)
    both = acc_ref[...] + jnp.dot(
        shard, weight_ref[...].reshape(2 * width, columns), preferred_element_type=jnp.float32
    )
    cosine, sine = cos_ref[...][None], sin_ref[...][None]

    def rotated(h):
        v = both[:, h * HD : (h + 1) * HD]
        turned = pltpu.roll(v, HD // 2, 1).reshape(-1, tokens, HD) * sine
        return (v.reshape(-1, tokens, HD) * cosine + turned).astype(jnp.bfloat16).reshape(rows, HD)

    scale = 1.0 / math.sqrt(HD)
    near = cache_ref.shape[0] // 2
    cache = cache_ref[:near] + cache_ref[near:]
    half = near // 2
    own_values = both[:, (heads + 1) * HD :].astype(jnp.bfloat16)
    keys = jnp.concatenate([cache[:half].reshape(PL, HD), rotated(heads)], 0)
    values = jnp.concatenate([cache[half:].reshape(PL, HD), own_values], 0)
    row = lax.broadcasted_iota(jnp.int32, (rows, rows), 0)
    col = lax.broadcasted_iota(jnp.int32, (rows, rows), 1)
    seen = (row // tokens == col // tokens) & (col <= row)
    nt = (((1,), (1,)), ((), ()))
    scores = [
        lax.dot_general(rotated(h), keys, nt, preferred_element_type=jnp.float32) * scale
        for h in range(heads)
    ]
    for h in range(heads):
        prior = scores[h][:, :PL]
        recent = jnp.where(seen, scores[h][:, PL:], -1e30)
        top = jnp.max(jnp.maximum(prior, recent), -1, keepdims=True)
        prior = jnp.exp(prior - top)
        recent = jnp.exp(recent - top)
        inverse = 1.0 / jnp.sum(prior + recent, -1, keepdims=True)
        weights = jnp.concatenate(
            [(prior * inverse).astype(jnp.bfloat16), (recent * inverse).astype(jnp.bfloat16)], -1
        )
        mixed = jnp.dot(weights, values, preferred_element_type=jnp.float32)
        attn_ref[:, h * HD : (h + 1) * HD] = mixed.astype(jnp.bfloat16)


def attend(acc, near, far, weights, cosine, sine, cache, tokens):
    rows, columns = acc.shape
    heads = columns // HD - 2
    return pl.pallas_call(
        functools.partial(attend_kernel, tokens),
        in_specs=[VMEM] * 7,
        out_specs=VMEM,
        out_shape=jax.ShapeDtypeStruct((rows, heads * HD), jnp.bfloat16),
        compiler_params=params(16),
        cost_estimate=pl.CostEstimate(
            flops=8 * heads * rows * PL * HD,
            bytes_accessed=4 * rows * heads * HD,
            transcendentals=2 * heads * rows * PL,
        ),
    )(acc, near, far, weights, cosine, sine, cache)


def fetch_kernel(shift, after_ref, near_hbm, far_hbm, wo_ref, sems):
    del after_ref
    copies = out_weight_copies(0, shift, near_hbm, far_hbm, wo_ref, sems)
    for copy in copies:
        copy.start()
    for copy in copies:
        copy.wait()


def fetch(shift, after, out_near, out_far):
    depth, width = out_near.shape[0], out_near.shape[1] // (CHIPS * CORES)
    return pl.pallas_call(
        functools.partial(fetch_kernel, shift),
        in_specs=[ANY] * 3,
        out_specs=VMEM,
        out_shape=jax.ShapeDtypeStruct((1, 2 * depth, width), jnp.bfloat16),
        scratch_shapes=[pltpu.SemaphoreType.DMA((2, 1))],
        compiler_params=params(8),
        cost_estimate=pl.CostEstimate(
            flops=0, bytes_accessed=8 * depth * width, transcendentals=0
        ),
    )(after, in_hbm(out_near), in_hbm(out_far))


def output_cost(count, rows, depth, width):
    return pl.CostEstimate(
        flops=2 * count * rows * depth * width,
        bytes_accessed=2 * count * depth * width,
        transcendentals=0,
    )


def output_halves_kernel(near_ref, far_ref, wo_ref, top_ref, bottom_ref):
    half = top_ref.shape[0]
    both = jnp.concatenate([near_ref[...], far_ref[...]], -1)
    block = jnp.dot(both, wo_ref[0], preferred_element_type=jnp.float32).astype(jnp.bfloat16)
    top_ref[...] = block[:half]
    bottom_ref[...] = block[half:]


def output_halves(near, far, weights):
    rows = near.shape[0]
    _, depth, width = weights.shape
    return pl.pallas_call(
        output_halves_kernel,
        in_specs=[VMEM] * 3,
        out_specs=[VMEM] * 2,
        out_shape=[jax.ShapeDtypeStruct((rows // 2, width), jnp.bfloat16)] * 2,
        compiler_params=params(8),
        cost_estimate=output_cost(1, rows, depth, width),
    )(near, far, weights)


def output_kernel(shifts, near_ref, far_ref, near_hbm, far_hbm, *refs):
    outs, (wo_ref, sems) = refs[:-2], refs[-2:]
    copies = [
        out_weight_copies(i, shift, near_hbm, far_hbm, wo_ref, sems)
        for i, shift in enumerate(shifts)
    ]
    for pair in copies:
        for copy in pair:
            copy.start()
    both = jnp.concatenate([near_ref[...], far_ref[...]], -1)
    for i, out_ref in enumerate(outs):
        for copy in copies[i]:
            copy.wait()
        out_ref[...] = jnp.dot(both, wo_ref[i], preferred_element_type=jnp.float32)


def output(near, far, shifts, out_near, out_far):
    rows = near.shape[0]
    depth, width = out_near.shape[0], out_near.shape[1] // (CHIPS * CORES)
    return pl.pallas_call(
        functools.partial(output_kernel, shifts),
        in_specs=[VMEM] * 2 + [ANY] * 2,
        out_specs=[VMEM] * len(shifts),
        out_shape=[jax.ShapeDtypeStruct((rows, width), jnp.float32)] * len(shifts),
        scratch_shapes=[
            pltpu.VMEM((len(shifts), 2 * depth, width), jnp.bfloat16),
            pltpu.SemaphoreType.DMA((2, len(shifts))),
        ],
        compiler_params=params(8),
        cost_estimate=output_cost(len(shifts), rows, 2 * depth, width),
    )(near, far, in_hbm(out_near), in_hbm(out_far))


def output_neighbours_kernel(near_ref, far_ref, near_hbm, far_hbm, *refs):
    above_late, above_early, below_early, below_late, wo_ref, sems = refs
    half = above_late.shape[0]
    copies = [
        out_weight_copies(i, shift, near_hbm, far_hbm, wo_ref, sems)
        for i, shift in enumerate((1, -1))
    ]
    for pair in copies:
        for copy in pair:
            copy.start()
    both = jnp.concatenate([near_ref[...], far_ref[...]], -1)
    for i, (top_ref, bottom_ref) in enumerate(((above_late, above_early), (below_early, below_late))):
        for copy in copies[i]:
            copy.wait()
        block = jnp.dot(both, wo_ref[i], preferred_element_type=jnp.float32)
        top_ref[...] = block[:half].astype(top_ref.dtype)
        bottom_ref[...] = block[half:].astype(bottom_ref.dtype)


def output_neighbours(near, far, out_near, out_far):
    rows = near.shape[0]
    depth, width = out_near.shape[0], out_near.shape[1] // (CHIPS * CORES)
    late = jax.ShapeDtypeStruct((rows // 2, width), jnp.float32)
    early = jax.ShapeDtypeStruct((rows // 2, width), jnp.bfloat16)
    return pl.pallas_call(
        output_neighbours_kernel,
        in_specs=[VMEM] * 2 + [ANY] * 2,
        out_specs=[VMEM] * 4,
        out_shape=[late, early, early, late],
        scratch_shapes=[
            pltpu.VMEM((2, 2 * depth, width), jnp.bfloat16),
            pltpu.SemaphoreType.DMA((2, 2)),
        ],
        compiler_params=params(8),
        cost_estimate=output_cost(2, rows, 2 * depth, width),
    )(near, far, in_hbm(out_near), in_hbm(out_far))


def pass_on_kernel(above_ref, below_ref, top_ref, bottom_ref, to_above_ref, to_below_ref):
    to_above_ref[...] = (above_ref[...] + top_ref[...].astype(jnp.float32)).astype(jnp.bfloat16)
    to_below_ref[...] = (below_ref[...] + bottom_ref[...].astype(jnp.float32)).astype(jnp.bfloat16)


def pass_on(above, below, top, bottom):
    block = jax.ShapeDtypeStruct(above.shape, jnp.bfloat16)
    return pl.pallas_call(
        pass_on_kernel,
        in_specs=[VMEM] * 4,
        out_specs=[VMEM] * 2,
        out_shape=[block, block],
        compiler_params=params(8),
    )(above, below, top, bottom)


def place_kernel(pick_ref, count_ref, mine_ref, *refs):
    parts, out_ref = [ref[...].astype(jnp.float32) for ref in refs[:-1]], refs[-1]
    half = mine_ref.shape[0] // 2
    top = mine_ref[:half] + parts[0] + parts[1]
    bottom = mine_ref[half:] + parts[2] + parts[3]
    total = jnp.concatenate([top, bottom], 0)
    slots, tokens, width = out_ref.shape
    picks = block_picks(pick_ref[...], slots, tokens, total.shape[0])
    placed = jnp.dot(picks, total.astype(jnp.bfloat16), preferred_element_type=jnp.float32)
    token = lax.broadcasted_iota(jnp.int32, (slots, tokens, width), 1)
    valid = token < count_ref[:, 0:1][:, None, :]
    out_ref[...] = jnp.where(valid, placed.reshape(slots, tokens, width), 0.0).astype(jnp.bfloat16)


def place(pick, count, mine, parts, slots, tokens):
    _, width = mine.shape
    return pl.pallas_call(
        place_kernel,
        in_specs=[VMEM] * (3 + len(parts)),
        out_specs=VMEM,
        out_shape=jax.ShapeDtypeStruct((slots, tokens, width), jnp.bfloat16),
        compiler_params=params(8),
    )(pick, count, mine, *parts)


def per_device(resp_rows, resp_len, resp_shard, group_prompt, prompt_kv, w_query, w_keyval, w_out):
    learners = lax.axis_size("seq")
    group = lax.axis_index("seq")
    group_size, tokens, width = resp_rows.shape
    rows = group_size * tokens

    near = learners // 2
    halves = [list(range(near)), list(range(near, learners))]
    pieces = prompt_kv.reshape(near, -1, HD)
    part = 16
    source = group_prompt - group // near * near
    held = (source >= 0) & (source < near)
    source = jnp.where(held, source, -near)[:, None] * part + jnp.arange(part)[None, :]
    prompts = source.reshape(-1)[:, None] == jnp.arange(near * part)[None, :]
    prompts = prompts.astype(jnp.bfloat16)
    pieces = lax.all_to_all(pieces, "seq", 0, 0, axis_index_groups=halves, tiled=True)

    x = resp_rows.reshape(rows, width)
    swap = lambda v: lax.ppermute(v, "tp", CORE_SWAP)
    below = lax.ppermute(x, "tp", chip_shift(1))
    above = lax.ppermute(x, "tp", chip_shift(-1))
    x_far = swap(x)
    x_last, below, above = lax.optimization_barrier((x, below, above))
    across = lax.ppermute(x_last, "tp", chip_shift(2))
    out_far = swap(w_out)
    shards = [x_far, below, swap(below), above, swap(above)]
    pieces, *shards = lax.optimization_barrier((pieces, *shards))
    cache = lax.all_to_all(route(prompts, pieces, learners), "seq", 0, 0, tiled=True)

    cosine, sine = rope_tables(tokens)
    acc, w_last = project(x, shards, w_query, w_keyval)
    attn = attend(acc, across, swap(across), w_last, cosine, sine, cache, tokens)
    resp_len, resp_shard, attn = lax.optimization_barrier((resp_len, resp_shard, attn))
    own_len = lax.dynamic_slice_in_dim(resp_len, group * group_size, group_size, 0)
    own_shard = lax.dynamic_slice_in_dim(resp_shard[:, 0], group * group_size, group_size, 0)
    match = own_shard[None, :] == jnp.arange(learners)[:, None]
    pick = jnp.max(jnp.where(match, jnp.arange(group_size)[None, :], -1), -1)
    count = jnp.max(jnp.where(match, own_len[None, :], 0), -1)
    spread = lambda v: jnp.broadcast_to(v[:, None], (learners, rows)).astype(jnp.int32)
    attn_far = swap(attn)
    w_across = fetch(2, attn, w_out, out_far)
    top, bottom = output_halves(attn, attn_far, w_across)
    top = lax.ppermute(top, "tp", chip_shift(1))
    bottom = lax.ppermute(bottom, "tp", chip_shift(-1))
    above_late, above_early, below_early, below_late = output_neighbours(
        attn, attn_far, w_out, out_far
    )
    above_early = lax.ppermute(above_early, "tp", chip_shift(1))
    below_early = lax.ppermute(below_early, "tp", chip_shift(-1))
    above_late, below_late = pass_on(above_late, below_late, top, bottom)
    (mine,) = output(attn, attn_far, (0,), w_out, out_far)
    parts = [
        lax.ppermute(above_late, "tp", chip_shift(1)),
        below_early,
        above_early,
        lax.ppermute(below_late, "tp", chip_shift(-1)),
    ]
    slots = place(spread(pick), spread(count), mine, parts, learners, tokens)
    return lax.all_to_all(slots, "seq", 0, 0, tiled=True)


def solution(mesh):
    return jax.shard_map(
        per_device,
        mesh=mesh,
        in_specs=(
            P("seq", None, "tp"),
            P(),
            P(),
            P(),
            P(None, "seq", None, "tp"),
            P(None, "tp"),
            P(None, None, "tp"),
            P("tp", None),
        ),
        out_specs=P("seq", None, "tp"),
        check_vma=False,
    )
```

```python
import functools
import math

import jax
import jax.numpy as jnp
from jax import lax
from jax.experimental import pallas as pl
from jax.experimental.pallas import tpu as pltpu
from jax.sharding import PartitionSpec as P

HD = 128
PL = 256
ROPE_BASE = 1000000.0
CHIPS = 4
CORES = 2


def chip_shift(step):
    return [
        (y * CORES + c, ((y + step) % CHIPS) * CORES + c) for y in range(CHIPS) for c in range(CORES)
    ]


CORE_SWAP = [(i, i ^ 1) for i in range(CHIPS * CORES)]


def rope_tables(count):
    places = (PL + jnp.arange(count)).astype(jnp.float32)
    freqs = ROPE_BASE ** (-(jnp.arange(HD // 2).astype(jnp.float32) * 2.0 / HD))
    angles = places[:, None] * freqs[None, :]
    cosine, sine = jnp.cos(angles), jnp.sin(angles)
    return jnp.concatenate([cosine, cosine], -1), jnp.concatenate([-sine, sine], -1)


VMEM = pl.BlockSpec(memory_space=pltpu.VMEM)
SMEM = pl.BlockSpec(memory_space=pltpu.SMEM)
ANY = pl.BlockSpec(memory_space=pl.ANY)


def in_hbm(x):
    return pltpu.with_memory_space_constraint(x, pltpu.HBM)


def params(mib):
    return pltpu.CompilerParams(vmem_limit_bytes=mib * 1024 * 1024)


def place_in_column(shifts, far):
    me = lax.axis_index("tp")
    y, c = me // CORES, me % CORES
    core = 1 - c if far else c
    return [((y + shift + CHIPS) % CHIPS) * CORES + core for shift in shifts]


def columns_at(index, width):
    return pl.ds(pl.multiple_of(index * width, width), width)


def block_picks(source, slots, size, rows):
    block = lax.broadcasted_iota(jnp.int32, (slots, rows), 1) // size
    row = lax.broadcasted_iota(jnp.int32, (slots, size, rows), 2) % size
    place = lax.broadcasted_iota(jnp.int32, (slots, size, rows), 1)
    chosen = jnp.where(block == source, 1.0, 0.0)[:, None, :]
    return jnp.where(row == place, chosen, 0.0).astype(jnp.bfloat16).reshape(-1, rows)


def route_kernel(pick_ref, piece_ref, out_ref):
    count, size, width = piece_ref.shape
    slots = out_ref.shape[0]
    part = pick_ref.shape[0] // slots
    for i in range(size // part):
        at = slice(i * part, (i + 1) * part)
        pieces = piece_ref[:, at, :].reshape(count * part, width)
        picked = jnp.dot(pick_ref[...], pieces, preferred_element_type=jnp.float32)
        out_ref[:, at, :] = picked.astype(jnp.bfloat16).reshape(slots, part, width)


def route(pick, pieces, slots):
    _, size, width = pieces.shape
    return pl.pallas_call(
        route_kernel,
        in_specs=[VMEM, VMEM],
        out_specs=VMEM,
        out_shape=jax.ShapeDtypeStruct((slots, size, width), pieces.dtype),
        compiler_params=params(8),
    )(pick, pieces)


def weight_row_copies(i, index, wq_hbm, wkv_hbm, weights, sems):
    width = weights.shape[1]
    first = wq_hbm.shape[1]
    at = columns_at(index, width)
    return (
        pltpu.make_async_copy(wq_hbm.at[at, :], weights.at[i, :, 0:first], sems.at[0, i]),
        pltpu.make_async_copy(
            wkv_hbm.at[0, at, :], weights.at[i, :, first : first + HD], sems.at[1, i]
        ),
        pltpu.make_async_copy(
            wkv_hbm.at[1, at, :], weights.at[i, :, first + HD : first + 2 * HD], sems.at[2, i]
        ),
    )


def project_pairs(rows_ref, weights, copies, later):
    _, width, columns = weights.shape
    total = None
    for pair in range(len(copies) // 2):
        for copy in copies[2 * pair] + copies[2 * pair + 1]:
            copy.wait()
        for group in later[pair] if pair < len(later) else ():
            for copy in group:
                copy.start()
        part = jnp.dot(
            rows_ref[:, 2 * pair * width : 2 * (pair + 1) * width],
            weights[2 * pair : 2 * (pair + 1)].reshape(2 * width, columns),
            preferred_element_type=jnp.float32,
        )
        total = part if total is None else total + part
    return total


def out_weight_copies(i, shift, near_hbm, far_hbm, wo_ref, sems):
    depth = near_hbm.shape[0]
    at = columns_at(place_in_column((shift,), False)[0], wo_ref.shape[2])
    return (
        pltpu.make_async_copy(near_hbm.at[:, at], wo_ref.at[i, 0:depth, :], sems.at[0, i]),
        pltpu.make_async_copy(far_hbm.at[:, at], wo_ref.at[i, depth : 2 * depth, :], sems.at[1, i]),
    )


def project_kernel(*refs):
    shards = refs[:6]
    wq_hbm, wkv_hbm, acc_ref, last_ref, rows_ref, weights, sems, last_sems, row_sems = refs[6:]
    width = weights.shape[1]
    near = place_in_column((0, -1, 1, 2), False)
    far = place_in_column((0, -1, 1, 2), True)
    order = [index for pair in zip(near, far) for index in pair]
    copies = [
        (
            pltpu.make_async_copy(
                shard, rows_ref.at[:, i * width : (i + 1) * width], row_sems.at[i]
            ),
            *weight_row_copies(i, index, wq_hbm, wkv_hbm, weights, sems),
        )
        for i, (shard, index) in enumerate(zip(shards, order))
    ]
    last = [
        weight_row_copies(i, index, wq_hbm, wkv_hbm, last_ref, last_sems)
        for i, index in enumerate(order[6:])
    ]
    for group in copies[:4]:
        for copy in group:
            copy.start()
    acc_ref[...] = project_pairs(rows_ref, weights, copies, [copies[4:], last])
    for group in last:
        for copy in group:
            copy.wait()


def project(x, shards, w_query, w_keyval):
    rows, width = x.shape
    columns = w_query.shape[1] + 2 * HD
    return pl.pallas_call(
        project_kernel,
        in_specs=[ANY] * 8,
        out_specs=[VMEM] * 2,
        out_shape=[
            jax.ShapeDtypeStruct((rows, columns), jnp.float32),
            jax.ShapeDtypeStruct((2, width, columns), jnp.bfloat16),
        ],
        scratch_shapes=[
            pltpu.VMEM((rows, 6 * width), jnp.bfloat16),
            pltpu.VMEM((6, width, columns), jnp.bfloat16),
            pltpu.SemaphoreType.DMA((3, 6)),
            pltpu.SemaphoreType.DMA((3, 2)),
            pltpu.SemaphoreType.DMA((6,)),
        ],
        compiler_params=params(16),
        cost_estimate=pl.CostEstimate(
            flops=2 * rows * 6 * width * columns,
            bytes_accessed=16 * width * columns,
            transcendentals=0,
        ),
    )(*[in_hbm(v) for v in (x, *shards, w_query, w_keyval)])


def finish_kernel(
    tokens, acc_ref, near_ref, far_ref, weight_ref, cos_ref, sin_ref, q_ref, k_ref, v_ref
):
    rows, columns = acc_ref.shape
    heads = columns // HD - 2
    width = near_ref.shape[1]
    shard = jnp.concatenate([near_ref[...], far_ref[...]], -1)
    both = acc_ref[...] + jnp.dot(
        shard, weight_ref[...].reshape(2 * width, columns), preferred_element_type=jnp.float32
    )
    cosine, sine = cos_ref[...][None], sin_ref[...][None]

    def rotated(h):
        v = both[:, h * HD : (h + 1) * HD]
        turned = pltpu.roll(v, HD // 2, 1).reshape(-1, tokens, HD) * sine
        return (v.reshape(-1, tokens, HD) * cosine + turned).astype(jnp.bfloat16).reshape(rows, HD)

    for h in range(heads):
        q_ref[h] = rotated(h)
    k_ref[...] = rotated(heads)
    v_ref[...] = both[:, (heads + 1) * HD :].astype(jnp.bfloat16)


def finish(acc, near, far, weights, cosine, sine, tokens):
    rows, columns = acc.shape
    heads = columns // HD - 2
    one = jax.ShapeDtypeStruct((rows, HD), jnp.bfloat16)
    return pl.pallas_call(
        functools.partial(finish_kernel, tokens),
        in_specs=[VMEM] * 6,
        out_specs=[VMEM] * 3,
        out_shape=[jax.ShapeDtypeStruct((heads, rows, HD), jnp.bfloat16), one, one],
        compiler_params=params(16),
    )(acc, near, far, weights, cosine, sine)


def attend_kernel(tokens, q_ref, k_ref, v_ref, cache_ref, attn_ref):
    heads, rows, _ = q_ref.shape
    scale = 1.0 / math.sqrt(HD)
    near = cache_ref.shape[0] // 2
    cache = cache_ref[:near] + cache_ref[near:]
    half = near // 2
    keys = jnp.concatenate([cache[:half].reshape(PL, HD), k_ref[...]], 0)
    values = jnp.concatenate([cache[half:].reshape(PL, HD), v_ref[...]], 0)
    row = lax.broadcasted_iota(jnp.int32, (rows, rows), 0)
    col = lax.broadcasted_iota(jnp.int32, (rows, rows), 1)
    seen = (row // tokens == col // tokens) & (col <= row)
    nt = (((1,), (1,)), ((), ()))
    scores = [
        lax.dot_general(q_ref[h], keys, nt, preferred_element_type=jnp.float32) * scale
        for h in range(heads)
    ]
    for h in range(heads):
        prior = scores[h][:, :PL]
        recent = jnp.where(seen, scores[h][:, PL:], -1e30)
        top = jnp.max(jnp.maximum(prior, recent), -1, keepdims=True)
        prior = jnp.exp(prior - top)
        recent = jnp.exp(recent - top)
        inverse = 1.0 / jnp.sum(prior + recent, -1, keepdims=True)
        weights = jnp.concatenate(
            [(prior * inverse).astype(jnp.bfloat16), (recent * inverse).astype(jnp.bfloat16)], -1
        )
        mixed = jnp.dot(weights, values, preferred_element_type=jnp.float32)
        attn_ref[:, h * HD : (h + 1) * HD] = mixed.astype(jnp.bfloat16)


def attend(queries, keys, values, cache, tokens):
    heads, rows, _ = queries.shape
    return pl.pallas_call(
        functools.partial(attend_kernel, tokens),
        in_specs=[VMEM] * 4,
        out_specs=VMEM,
        out_shape=jax.ShapeDtypeStruct((rows, heads * HD), jnp.bfloat16),
        compiler_params=params(16),
        cost_estimate=pl.CostEstimate(
            flops=8 * heads * rows * PL * HD,
            bytes_accessed=4 * rows * heads * HD,
            transcendentals=2 * heads * rows * PL,
        ),
    )(queries, keys, values, cache)


def fetch_kernel(shift, after_ref, near_hbm, far_hbm, wo_ref, sems):
    del after_ref
    copies = out_weight_copies(0, shift, near_hbm, far_hbm, wo_ref, sems)
    for copy in copies:
        copy.start()
    for copy in copies:
        copy.wait()


def fetch(shift, after, out_near, out_far):
    depth, width = out_near.shape[0], out_near.shape[1] // (CHIPS * CORES)
    return pl.pallas_call(
        functools.partial(fetch_kernel, shift),
        in_specs=[ANY] * 3,
        out_specs=VMEM,
        out_shape=jax.ShapeDtypeStruct((1, 2 * depth, width), jnp.bfloat16),
        scratch_shapes=[pltpu.SemaphoreType.DMA((2, 1))],
        compiler_params=params(8),
        cost_estimate=pl.CostEstimate(
            flops=0, bytes_accessed=8 * depth * width, transcendentals=0
        ),
    )(after, in_hbm(out_near), in_hbm(out_far))


def output_cost(count, rows, depth, width):
    return pl.CostEstimate(
        flops=2 * count * rows * depth * width,
        bytes_accessed=2 * count * depth * width,
        transcendentals=0,
    )


def output_halves_kernel(near_ref, far_ref, wo_ref, top_ref, bottom_ref):
    half = top_ref.shape[0]
    both = jnp.concatenate([near_ref[...], far_ref[...]], -1)
    block = jnp.dot(both, wo_ref[0], preferred_element_type=jnp.float32).astype(jnp.bfloat16)
    top_ref[...] = block[:half]
    bottom_ref[...] = block[half:]


def output_halves(near, far, weights):
    rows = near.shape[0]
    _, depth, width = weights.shape
    return pl.pallas_call(
        output_halves_kernel,
        in_specs=[VMEM] * 3,
        out_specs=[VMEM] * 2,
        out_shape=[jax.ShapeDtypeStruct((rows // 2, width), jnp.bfloat16)] * 2,
        compiler_params=params(8),
        cost_estimate=output_cost(1, rows, depth, width),
    )(near, far, weights)


def output_kernel(shifts, near_ref, far_ref, near_hbm, far_hbm, *refs):
    outs, (wo_ref, sems) = refs[:-2], refs[-2:]
    copies = [
        out_weight_copies(i, shift, near_hbm, far_hbm, wo_ref, sems)
        for i, shift in enumerate(shifts)
    ]
    for pair in copies:
        for copy in pair:
            copy.start()
    both = jnp.concatenate([near_ref[...], far_ref[...]], -1)
    for i, out_ref in enumerate(outs):
        for copy in copies[i]:
            copy.wait()
        out_ref[...] = jnp.dot(both, wo_ref[i], preferred_element_type=jnp.float32)


def output(near, far, shifts, out_near, out_far):
    rows = near.shape[0]
    depth, width = out_near.shape[0], out_near.shape[1] // (CHIPS * CORES)
    return pl.pallas_call(
        functools.partial(output_kernel, shifts),
        in_specs=[VMEM] * 2 + [ANY] * 2,
        out_specs=[VMEM] * len(shifts),
        out_shape=[jax.ShapeDtypeStruct((rows, width), jnp.float32)] * len(shifts),
        scratch_shapes=[
            pltpu.VMEM((len(shifts), 2 * depth, width), jnp.bfloat16),
            pltpu.SemaphoreType.DMA((2, len(shifts))),
        ],
        compiler_params=params(8),
        cost_estimate=output_cost(len(shifts), rows, 2 * depth, width),
    )(near, far, in_hbm(out_near), in_hbm(out_far))


def output_neighbours_kernel(near_ref, far_ref, near_hbm, far_hbm, *refs):
    above_late, above_early, below_early, below_late, wo_ref, sems = refs
    half = above_late.shape[0]
    copies = [
        out_weight_copies(i, shift, near_hbm, far_hbm, wo_ref, sems)
        for i, shift in enumerate((1, -1))
    ]
    for pair in copies:
        for copy in pair:
            copy.start()
    both = jnp.concatenate([near_ref[...], far_ref[...]], -1)
    for i, (top_ref, bottom_ref) in enumerate(((above_late, above_early), (below_early, below_late))):
        for copy in copies[i]:
            copy.wait()
        block = jnp.dot(both, wo_ref[i], preferred_element_type=jnp.float32)
        top_ref[...] = block[:half].astype(top_ref.dtype)
        bottom_ref[...] = block[half:].astype(bottom_ref.dtype)


def output_neighbours(near, far, out_near, out_far):
    rows = near.shape[0]
    depth, width = out_near.shape[0], out_near.shape[1] // (CHIPS * CORES)
    late = jax.ShapeDtypeStruct((rows // 2, width), jnp.float32)
    early = jax.ShapeDtypeStruct((rows // 2, width), jnp.bfloat16)
    return pl.pallas_call(
        output_neighbours_kernel,
        in_specs=[VMEM] * 2 + [ANY] * 2,
        out_specs=[VMEM] * 4,
        out_shape=[late, early, early, late],
        scratch_shapes=[
            pltpu.VMEM((2, 2 * depth, width), jnp.bfloat16),
            pltpu.SemaphoreType.DMA((2, 2)),
        ],
        compiler_params=params(8),
        cost_estimate=output_cost(2, rows, 2 * depth, width),
    )(near, far, in_hbm(out_near), in_hbm(out_far))


def pass_on_kernel(above_ref, below_ref, top_ref, bottom_ref, to_above_ref, to_below_ref):
    to_above_ref[...] = (above_ref[...] + top_ref[...].astype(jnp.float32)).astype(jnp.bfloat16)
    to_below_ref[...] = (below_ref[...] + bottom_ref[...].astype(jnp.float32)).astype(jnp.bfloat16)


def pass_on(above, below, top, bottom):
    block = jax.ShapeDtypeStruct(above.shape, jnp.bfloat16)
    return pl.pallas_call(
        pass_on_kernel,
        in_specs=[VMEM] * 4,
        out_specs=[VMEM] * 2,
        out_shape=[block, block],
        compiler_params=params(8),
    )(above, below, top, bottom)


def place_kernel(pick_ref, count_ref, mine_ref, *refs):
    parts, out_ref = [ref[...].astype(jnp.float32) for ref in refs[:-1]], refs[-1]
    half = mine_ref.shape[0] // 2
    top = mine_ref[:half] + parts[0] + parts[1]
    bottom = mine_ref[half:] + parts[2] + parts[3]
    total = jnp.concatenate([top, bottom], 0)
    slots, tokens, width = out_ref.shape
    picks = block_picks(pick_ref[...], slots, tokens, total.shape[0])
    placed = jnp.dot(picks, total.astype(jnp.bfloat16), preferred_element_type=jnp.float32)
    token = lax.broadcasted_iota(jnp.int32, (slots, tokens, width), 1)
    valid = token < count_ref[:, 0:1][:, None, :]
    out_ref[...] = jnp.where(valid, placed.reshape(slots, tokens, width), 0.0).astype(jnp.bfloat16)


def place(pick, count, mine, parts, slots, tokens):
    _, width = mine.shape
    return pl.pallas_call(
        place_kernel,
        in_specs=[VMEM] * (3 + len(parts)),
        out_specs=VMEM,
        out_shape=jax.ShapeDtypeStruct((slots, tokens, width), jnp.bfloat16),
        compiler_params=params(8),
    )(pick, count, mine, *parts)


def per_device(resp_rows, resp_len, resp_shard, group_prompt, prompt_kv, w_query, w_keyval, w_out):
    learners = lax.axis_size("seq")
    group = lax.axis_index("seq")
    group_size, tokens, width = resp_rows.shape
    rows = group_size * tokens

    near = learners // 2
    halves = [list(range(near)), list(range(near, learners))]
    pieces = prompt_kv.reshape(near, -1, HD)
    part = 16
    source = group_prompt - group // near * near
    held = (source >= 0) & (source < near)
    source = jnp.where(held, source, -near)[:, None] * part + jnp.arange(part)[None, :]
    prompts = source.reshape(-1)[:, None] == jnp.arange(near * part)[None, :]
    prompts = prompts.astype(jnp.bfloat16)
    pieces = lax.all_to_all(pieces, "seq", 0, 0, axis_index_groups=halves, tiled=True)

    x = resp_rows.reshape(rows, width)
    swap = lambda v: lax.ppermute(v, "tp", CORE_SWAP)
    below = lax.ppermute(x, "tp", chip_shift(1))
    above = lax.ppermute(x, "tp", chip_shift(-1))
    x_far = swap(x)
    x_last, below, above = lax.optimization_barrier((x, below, above))
    across = lax.ppermute(x_last, "tp", chip_shift(2))
    out_far = swap(w_out)
    shards = [x_far, below, swap(below), above, swap(above)]
    pieces, *shards = lax.optimization_barrier((pieces, *shards))
    cache = lax.all_to_all(route(prompts, pieces, learners), "seq", 0, 0, tiled=True)

    cosine, sine = rope_tables(tokens)
    acc, w_last = project(x, shards, w_query, w_keyval)
    projected = finish(acc, across, swap(across), w_last, cosine, sine, tokens)
    attn = attend(*projected, cache, tokens)
    resp_len, resp_shard, attn = lax.optimization_barrier((resp_len, resp_shard, attn))
    own_len = lax.dynamic_slice_in_dim(resp_len, group * group_size, group_size, 0)
    own_shard = lax.dynamic_slice_in_dim(resp_shard[:, 0], group * group_size, group_size, 0)
    match = own_shard[None, :] == jnp.arange(learners)[:, None]
    pick = jnp.max(jnp.where(match, jnp.arange(group_size)[None, :], -1), -1)
    count = jnp.max(jnp.where(match, own_len[None, :], 0), -1)
    spread = lambda v: jnp.broadcast_to(v[:, None], (learners, rows)).astype(jnp.int32)
    attn_far = swap(attn)
    w_across = fetch(2, attn, w_out, out_far)
    top, bottom = output_halves(attn, attn_far, w_across)
    top = lax.ppermute(top, "tp", chip_shift(1))
    bottom = lax.ppermute(bottom, "tp", chip_shift(-1))
    above_late, above_early, below_early, below_late = output_neighbours(
        attn, attn_far, w_out, out_far
    )
    above_early = lax.ppermute(above_early, "tp", chip_shift(1))
    below_early = lax.ppermute(below_early, "tp", chip_shift(-1))
    above_late, below_late = pass_on(above_late, below_late, top, bottom)
    (mine,) = output(attn, attn_far, (0,), w_out, out_far)
    parts = [
        lax.ppermute(above_late, "tp", chip_shift(1)),
        below_early,
        above_early,
        lax.ppermute(below_late, "tp", chip_shift(-1)),
    ]
    slots = place(spread(pick), spread(count), mine, parts, learners, tokens)
    return lax.all_to_all(slots, "seq", 0, 0, tiled=True)


def solution(mesh):
    return jax.shard_map(
        per_device,
        mesh=mesh,
        in_specs=(
            P("seq", None, "tp"),
            P(),
            P(),
            P(),
            P(None, "seq", None, "tp"),
            P(None, "tp"),
            P(None, None, "tp"),
            P("tp", None),
        ),
        out_specs=P("seq", None, "tp"),
        check_vma=False,
    )
```
